128 devices in a mesh: tm: 8 (over y, core), sx: 4 (over z), sy: 4 (over x).
Axes of the slice: x: 4, y: 4, z: 4, core: 2. Of those that a mesh axis runs over, the one named last changes fastest.
Arguments:
- initial: float32 [512, 1536], P('sx', 'sy'), may hold values from -6 to 6
- guesses: float32 [8, 512, 1536], P('tm', 'sx', 'sy'), may hold values from -6 to 6
- conduct: float32 [512, 1536], P('sx', 'sy'), may hold values from 0.25 to 4
- source: float32 [512, 1536], P('sx', 'sy'), may hold values from -6 to 6
Outputs:
- corrected: float32 [8, 512, 1536], P('tm', 'sx', 'sy')
The draws below stay inside these ranges and needn't reach their ends.
All inputs are finite; a program needn't handle non-finite values.
Results may differ from the reference program's by a relative error of at most 0.00002.
Values sent between devices are 32-bit elements; how exact they have to be, the bound alone decides.
A program may use at most 128 MiB of HBM per device.

```python
import math
from functools import partial
import jax
import jax.numpy as jnp
from jax import lax

FINE = 4
NX = 512
NY = 1536
NC = 8


def shard_levels(key, shape, pieces, smallest, top_value):
    level, own = 1.0, jax.random.fold_in(key, 6)
    for position, blocks in pieces:
        draws = jnp.exp(jax.random.uniform(jax.random.fold_in(own, position), (blocks,), jnp.float32, smallest / len(pieces), top_value / len(pieces)))
        level = level * jnp.repeat(draws, shape[position] // blocks).reshape([-1 if axis == position else 1 for axis in range(len(shape))])
    return level


def gaussian(rng, dims, width, most, shards=(), dtype=jnp.bfloat16):
    array = width * jax.random.normal(rng, dims, jnp.float32)
    if shards:
        array = array * shard_levels(rng, dims, shards, -0.22, 0.18)
    return jnp.clip(array, -most, most).astype(dtype)


def setup_inputs(seed: int = 0) -> dict:
    streams_of = jax.random.split(jax.random.key(seed), 5)
    initial = gaussian(streams_of[0], (NX, NY), 1.0, 6.0, ((0, 4), (1, 4)), jnp.float32)
    guesses = gaussian(streams_of[1], (NC, NX, NY), 1.0, 6.0, ((0, 8), (1, 4), (2, 4)), jnp.float32)
    conduct = jnp.clip(jnp.exp(math.log(4.0) - 2.7725887 * jax.random.uniform(streams_of[2], (NX, NY), jnp.float32) ** shard_levels(streams_of[2], (NX, NY), ((0, 4), (1, 4)), -0.2, 0.2)), 0.25, 4.0)
    source = gaussian(streams_of[3], (NX, NY), 1.0, 6.0, ((0, 4), (1, 4)), jnp.float32)
    return dict(initial=initial, guesses=guesses, conduct=conduct, source=source)


TIME_STEP = 0.035
NONLINEAR_GAIN = 0.5


def conductance(values, factor):
    return factor * (1.0 + NONLINEAR_GAIN * jnp.tanh(values))


def divergence(v_ext, c_ext, source, inv_area):
    k_ext = conductance(v_ext, c_ext)
    centre = v_ext[..., 1:-1, 1:-1]
    k_mid = k_ext[..., 1:-1, 1:-1]
    accrued = 0.5 * (k_mid + k_ext[..., 2:, 1:-1]) * (v_ext[..., 2:, 1:-1] - centre)
    accrued = accrued + 0.5 * (k_mid + k_ext[..., :-2, 1:-1]) * (v_ext[..., :-2, 1:-1] - centre)
    accrued = accrued + 0.5 * (k_mid + k_ext[..., 1:-1, 2:]) * (v_ext[..., 1:-1, 2:] - centre)
    accrued = accrued + 0.5 * (k_mid + k_ext[..., 1:-1, :-2]) * (v_ext[..., 1:-1, :-2] - centre)
    return accrued * inv_area + source


def restrict(field_in):
    leading = field_in.shape[:-2]
    height, breadth = field_in.shape[-2], field_in.shape[-1]
    blocks = field_in.reshape(leading + (height // 2, 2, breadth // 2, 2))
    return 0.25 * (blocks[..., :, 0, :, 0] + blocks[..., :, 0, :, 1] + blocks[..., :, 1, :, 0] + blocks[..., :, 1, :, 1])


def prolong(field_in):
    return jnp.repeat(jnp.repeat(field_in, 2, axis=-2), 2, axis=-1)


def pad_cells(field_in):
    widths = [(0, 0)] * (field_in.ndim - 2) + [(1, 1), (1, 1)]
    return jnp.pad(field_in, widths)


def advance(present, conduct, source, inv_area, step_len):
    conduct_ext = pad_cells(conduct)
    slope_one = divergence(pad_cells(present), conduct_ext, source, inv_area)
    section_value = present + step_len * slope_one
    slope_two = divergence(pad_cells(section_value), conduct_ext, source, inv_area)
    return 0.5 * ((present + section_value) + step_len * slope_two)


def fine_interval(present, conduct, source):
    for repeat_index in range(FINE):
        present = advance(present, conduct, source, 1.0, TIME_STEP)
    return present


def reference(initial, guesses, conduct, source):
    coarse_conduct = restrict(conduct)
    coarse_source = restrict(source)
    runner = partial(fine_interval, conduct=conduct, source=source)
    starts = jnp.concatenate([initial[None], guesses[:-1]], axis=0)
    relaxed = lax.map(runner, starts)
    again = jnp.concatenate([initial[None], relaxed[:-1]], axis=0)
    propagated = lax.map(runner, again)
    targets = restrict(propagated) - advance(restrict(again), coarse_conduct, coarse_source, 0.25, TIME_STEP * FINE)

    def chain(carried, target):
        following = advance(carried[None], coarse_conduct, coarse_source, 0.25, TIME_STEP * FINE)[0] + target
        return following, following

    anchor = restrict(initial)
    final_state, coarse = lax.scan(chain, anchor, targets)
    return relaxed + prolong(coarse - restrict(relaxed))
```

```python
import jax
import jax.numpy as jnp
from jax import lax
from jax.experimental import pallas as pl
from jax.experimental.pallas import tpu as pltpu
from jax.sharding import PartitionSpec as P

MESH = pl.DeviceIdType.MESH
FINE = 4
TIME_STEP = 0.035

ROWS, COLS, HALO = 128, 384, 16
EXT = ROWS + 2 * HALO
T_FINE = EXT // 8
T_COARSE = T_FINE // 2
CROWS = ROWS // 2
T_CHAIN = (CROWS + 32) // 8
LOW, HIGH = 16, 112
OWN, FROM_N, FROM_S, FROM_L, FROM_R, FROM_NL, FROM_NR, FROM_SL, FROM_SR = range(9)


def roll(x, shift, axis):
    shift = shift % x.shape[axis]
    return pltpu.roll(x, shift, axis) if shift else x


def flux_pass(src, coef, drift, T, W, emit):
    def load(t):
        values = [src[t, w] for w in range(W)]
        return values, [coef[t, w] * (2.0 + jnp.tanh(values[w])) for w in range(W)]

    def flux(v, k, vn, kn):
        return (k + kn) * (vn - v)

    first, last = load(0), load(T - 1)
    final = [flux(last[0][w], last[1][w], roll(first[0][w], -1, 0), roll(first[1][w], -1, 0)) for w in range(W)]
    above = [roll(f, 1, 0) for f in final]
    here = first
    for t in range(T):
        v, k = here
        if t < T - 1:
            following = last if t + 1 == T - 1 else load(t + 1)
            below = [flux(v[w], k[w], following[0][w], following[1][w]) for w in range(W)]
        else:
            following, below = None, final
        east = [flux(v[w], k[w], v[w + 1], k[w + 1]) for w in range(W - 1)]
        east.append(flux(v[W - 1], k[W - 1], roll(v[0], -1, 1), roll(k[0], -1, 1)))
        west = [roll(east[W - 1], 1, 1)] + east[:-1]
        for w in range(W):
            total = (v[w] + drift[t, w]) + ((east[w] - west[w]) + (below[w] - above[w]))
            emit(t, w, v[w], total)
        here, above = following, below


def heun(state, section, coef, drift, T, W, lanes, row_masks, emit=None):
    def keep(t, w, x):
        if w in (0, W - 1):
            x = x * lanes
        if t in row_masks:
            x = x * row_masks[t]
        return x

    def first(t, w, value, total):
        section[t, w] = keep(t, w, total)

    def second(t, w, value, total):
        result = keep(t, w, 0.5 * (state[t, w] + total))
        if emit is None:
            state[t, w] = result
        else:
            emit(t, w, result)

    flux_pass(state, coef, drift, T, W, first)
    flux_pass(section, coef, drift, T, W, second)


def pieces(x):
    top = x.astype(jnp.bfloat16)
    rest = x - top.astype(jnp.float32)
    middle = rest.astype(jnp.bfloat16)
    low = (rest - middle.astype(jnp.float32)).astype(jnp.bfloat16)
    return top, middle, low


def move_columns(x, choice):
    top, middle, low = [jnp.dot(part, choice, preferred_element_type=jnp.float32) for part in pieces(x)]
    return (top + middle) + low


def kernel(
    initial, guesses, conduct, source, out,
    X, Y, PS, PR, V, A, CH, SD, SPREAD, GATHER, RN, RX, RV, CA, CC, CSD, NAT, PK, E, PE, V12, A12, C12, S12, CN, CB, OUT,
    load_sem, store_sem, send1, recv1, send_relaxed, recv_relaxed, send3, recv3, send_coef, send_share, recv_share, ready,
):
    nt, nx, ny = lax.axis_size("tm"), lax.axis_size("sx"), lax.axis_size("sy")
    me, row, col = lax.axis_index("tm"), lax.axis_index("sx"), lax.axis_index("sy")
    chip, core = me // 2, lax.rem(me, 2)
    last = nt - 1
    north, south = lax.rem(row + nx - 1, nx), lax.rem(row + 1, nx)
    left, right = lax.rem(col + ny - 1, ny), lax.rem(col + 1, ny)
    spatial = [(north, col), (south, col), (row, left), (row, right),
               (north, left), (north, right), (south, left), (south, right)]

    barrier = pltpu.get_barrier_semaphore()
    for r, c in spatial:
        pl.semaphore_signal(barrier, inc=1, device_id=(me, r, c), device_id_type=MESH)
    for step in range(1, nt):
        pl.semaphore_signal(barrier, inc=1, device_id=(lax.rem(me + step, nt), row, col), device_id_type=MESH)

    def own_load(field, ref):
        return pltpu.make_async_copy(ref, X.at[field, HALO:HALO + ROWS, 0:COLS], load_sem.at[field])

    @pl.when(me == last)
    def _():
        own_load(0, initial).start()

    @pl.when(me != last)
    def _():
        own_load(0, guesses.at[0]).start()

    own_load(1, conduct).start()
    own_load(2, source).start()

    lane = lax.broadcasted_iota(jnp.int32, (8, 128), 1)
    sublane = lax.broadcasted_iota(jnp.int32, (8, 128), 0)
    one, zero = jnp.ones((8, 128), jnp.float32), jnp.zeros((8, 128), jnp.float32)
    at_top, at_bottom, at_left, at_right = row == 0, row == nx - 1, col == 0, col == ny - 1
    in_lanes = jnp.where(jnp.logical_or(jnp.logical_and(lane < LOW, at_left), jnp.logical_and(lane >= HIGH, at_right)), zero, one)

    def strip_mask(which, edge):
        return jnp.where(jnp.logical_and(sublane == which, edge), zero, one)

    n = lax.broadcasted_iota(jnp.int32, (512, 512), 0)
    o = lax.broadcasted_iota(jnp.int32, (512, 512), 1)
    place = (o & 127) * 4 + (o >> 7)
    from_n = jnp.where(n < COLS, n + 64, jnp.where(n < COLS + HALO, n + 64, jnp.where(n >= 512 - HALO, n - 448, -1)))
    SPREAD[...] = jnp.where(place == from_n, 1.0, 0.0).astype(jnp.bfloat16)
    n = lax.broadcasted_iota(jnp.int32, (512, COLS), 1)
    o = lax.broadcasted_iota(jnp.int32, (512, COLS), 0)
    GATHER[...] = jnp.where((o & 127) * 4 + (o >> 7) == n + 64, 1.0, 0.0).astype(jnp.bfloat16)

    pl.semaphore_wait(barrier, 8 + nt - 1)

    def row_copy(field, ref, side):
        where = (north, col) if side == 0 else (south, col)
        src = ref.at[0:HALO, :] if side == 0 else ref.at[ROWS - HALO:ROWS, :]
        dst = X.at[field, HALO + ROWS:EXT, 0:COLS] if side == 0 else X.at[field, 0:HALO, 0:COLS]
        k = field * 2 + side
        return pltpu.make_async_remote_copy(src, dst, send1.at[k], recv1.at[k], (me,) + where, MESH)

    @pl.when(me == last)
    def _():
        for side in range(2):
            row_copy(0, initial, side).start()

    @pl.when(me != last)
    def _():
        for side in range(2):
            row_copy(0, guesses.at[0], side).start()

    for field, ref in ((1, conduct), (2, source)):
        for side in range(2):
            row_copy(field, ref, side).start()

    group = lane // 16
    for field in range(3):
        own_load(field, conduct).wait()
        for side in range(2):
            for half in range(2):
                packed = None
                for q in range(8):
                    r0 = HALO + 64 * half + 8 * q
                    block = X[field, r0:r0 + 8, 0:128] if side == 0 else X[field, r0:r0 + 8, COLS - 128:COLS]
                    block = roll(block, 16 * q if side == 0 else 16 * q + 16, 1)
                    packed = block if packed is None else jnp.where(group == q, block, packed)
                PS[side, half, field] = packed

    def column_copies():
        plan = [
            (PS.at[1], PR.at[0:2], 6, (row, right)),
            (PS.at[0], PR.at[2:4], 7, (row, left)),
            (PS.at[1, 1], PR.at[4], 8, (south, right)),
            (PS.at[0, 1], PR.at[5], 9, (south, left)),
            (PS.at[1, 0], PR.at[6], 10, (north, right)),
            (PS.at[0, 0], PR.at[7], 11, (north, left)),
        ]
        return [pltpu.make_async_remote_copy(s, d, send1.at[k], recv1.at[k], (me,) + w, MESH) for s, d, k, w in plan]

    for copy in column_copies():
        copy.start()
    for copy in column_copies():
        copy.wait_recv()
    for field in range(3):
        for side in range(2):
            row_copy(field, conduct, side).wait_recv()

    for step in range(1, nt):
        pl.semaphore_signal(ready, inc=1, device_id=(lax.rem(me + step, nt), row, col), device_id_type=MESH)

    for field in range(3):
        for e in range(EXT // 8):
            if e < 2:
                from_left, from_right, q = PR[4, field], PR[5, field], 6 + e
            elif e >= 18:
                from_left, from_right, q = PR[6, field], PR[7, field], e - 18
            else:
                half, q = (e - 2) // 8, (e - 2) % 8
                from_left, from_right = PR[half, field], PR[2 + half, field]
            value = jnp.where(lane < 64, roll(from_right, -16 * q, 1), roll(from_left, 112 - 16 * q, 1))
            X[field, 8 * e:8 * e + 8, COLS:512] = value

    top16, bottom16 = strip_mask(0, at_top), strip_mask(7, at_bottom)

    def fine_mask(t):
        m = in_lanes
        if t < HALO:
            m = m * top16
        if t >= T_FINE - HALO:
            m = m * bottom16
        return m

    for field, dest, factor in ((0, V, 1.0), (1, CH, 0.25 * TIME_STEP), (2, SD, TIME_STEP)):
        spread = move_columns(X[field], SPREAD[...])
        for w in range(4):
            Y[w] = spread[:, 128 * w:128 * w + 128]
        for t in range(T_FINE):
            m = fine_mask(t) * factor
            for w in range(4):
                dest[t, w] = Y[w, pl.ds(t, 8, stride=T_FINE), :] * m

    def four(ref, t, w):
        return (ref[2 * t, 2 * w] + ref[2 * t, 2 * w + 1]) + (ref[2 * t + 1, 2 * w] + ref[2 * t + 1, 2 * w + 1])

    def pack_coarse(slot):
        eighth = lane // 8
        for side in range(2):
            packed = None
            for rb in range(8):
                for w in range(2):
                    q = rb * 2 + w
                    block = NAT[slot, w, 8 + 8 * rb:16 + 8 * rb, :]
                    block = roll(block, 8 * q - LOW if side == 0 else 8 * q - (HIGH - 8), 1)
                    packed = block if packed is None else jnp.where(eighth == q, block, packed)
            PK[slot, side] = packed

    def coarse_copies(source_slot, slot, tm, sems):
        nat, pk = NAT.at[source_slot], PK.at[source_slot]
        plan = [
            (nat.at[:, 8:8 + CROWS, :], E.at[slot, :, 16:16 + CROWS, :], OWN, (row, col)),
            (nat.at[:, CROWS - 8:CROWS + 8, :], E.at[slot, :, 0:16, :], FROM_N, (south, col)),
            (nat.at[:, 8:24, :], E.at[slot, :, 16 + CROWS:32 + CROWS, :], FROM_S, (north, col)),
            (pk.at[1], PE.at[slot, FROM_L], FROM_L, (row, right)),
            (pk.at[0], PE.at[slot, FROM_R], FROM_R, (row, left)),
            (pk.at[1], PE.at[slot, FROM_NL], FROM_NL, (south, right)),
            (pk.at[0], PE.at[slot, FROM_NR], FROM_NR, (south, left)),
            (pk.at[1], PE.at[slot, FROM_SL], FROM_SL, (north, right)),
            (pk.at[0], PE.at[slot, FROM_SR], FROM_SR, (north, left)),
        ]
        return [pltpu.make_async_remote_copy(s, d, sems.at[k], recv3.at[slot, k], (tm,) + w, MESH) for s, d, k, w in plan]

    for t in range(T_COARSE):
        for w in range(2):
            c, s = 0.25 * four(CH, t, w), four(SD, t, w)
            CC[t, w] = c
            CSD[t, w] = s
            NAT[1, w, pl.ds(t, 8, stride=T_COARSE), :] = c
            NAT[2, w, pl.ds(t, 8, stride=T_COARSE), :] = s
    for k in (1, 2):
        pack_coarse(k)
        for copy in coarse_copies(k, 6 + k, me, send_coef.at[k - 1])[1:]:
            copy.start()
        for w in range(2):
            E[6 + k, w, 16:16 + CROWS, :] = NAT[k, w, 8:8 + CROWS, :]

    fine_rows = {HALO - 1: top16, T_FINE - HALO: bottom16}

    def fine_run():
        def body(i, carry):
            heun(V, A, CH, SD, T_FINE, 4, in_lanes, fine_rows)
            return carry

        lax.fori_loop(0, FINE, body, 0)

    fine_run()

    for t in range(T_FINE):
        for w in range(4):
            RN[w, pl.ds(t, 8, stride=T_FINE), :] = V[t, w]
    relaxed_copy = pltpu.make_async_remote_copy(
        RN.at[:, HALO:HALO + ROWS, :], RX, send_relaxed, recv_relaxed, (lax.rem(me + 1, nt), row, col), MESH)
    relaxed_copy.start()
    for t in range(T_COARSE):
        for w in range(2):
            RV[t, w] = 0.25 * four(V, t, w)

    fine_run()

    share_of_psi = jnp.where(me == last, 0.0, 1.0)

    def target(t, w, result):
        NAT[0, w, pl.ds(t, 8, stride=T_COARSE), :] = 0.25 * four(V, t, w) - share_of_psi * result

    coarse_rows = {HALO // 2 - 1: top16, T_COARSE - HALO // 2: bottom16}
    heun(RV, CA, CC, CSD, T_COARSE, 2, in_lanes, coarse_rows, target)
    pack_coarse(0)
    pl.semaphore_wait(ready, nt - 1)

    slot_out = jnp.where(me == last, 0, me + 1)

    def each_receiver(action):
        for chip_to in range(nt // 2):
            wanted = jnp.logical_or(me == last, jnp.logical_and(chip_to > chip, me < last - 1))
            copies = coarse_copies(0, slot_out, 2 * chip_to + 1, send3.at[chip_to])

            @pl.when(wanted)
            def _():
                if chip_to == nt // 2 - 1:
                    @pl.when(me != last)
                    def _():
                        action(copies[0])
                else:
                    action(copies[0])
                for copy in copies[1:]:
                    action(copy)

    each_receiver(lambda copy: copy.start())

    def unpack(slot, store):
        for rb in range(12):
            if rb < 2:
                from_left, from_right, own = PE[slot, FROM_NL], PE[slot, FROM_NR], 6 + rb
            elif rb >= 10:
                from_left, from_right, own = PE[slot, FROM_SL], PE[slot, FROM_SR], rb - 10
            else:
                from_left, from_right, own = PE[slot, FROM_L], PE[slot, FROM_R], rb - 2
            for w in range(2):
                q = own * 2 + w
                value = E[slot, w, 8 * rb:8 * rb + 8, :]
                value = jnp.where(lane < LOW, roll(from_left, LOW - 8 - 8 * q, 1), value)
                value = jnp.where(lane >= HIGH, roll(from_right, HIGH - 8 * q, 1), value)
                mask = in_lanes
                if rb < 2:
                    mask = mask * jnp.where(at_top, 0.0, 1.0)
                if rb >= 10:
                    mask = mask * jnp.where(at_bottom, 0.0, 1.0)
                E[slot, w, 8 * rb:8 * rb + 8, :] = value * mask
        for t in range(T_CHAIN):
            for w in range(2):
                store(t, w, E[slot, w, pl.ds(t, 8, stride=T_CHAIN), :])

    def await_slot(slot, own=True):
        copies = coarse_copies(0, slot, me, send3.at[0])
        for copy in copies if own else copies[1:]:
            copy.wait_recv()

    chain_rows = {15 % T_CHAIN: strip_mask(15 // T_CHAIN, at_top), 80 % T_CHAIN: strip_mask(80 // T_CHAIN, at_bottom)}

    for slot in (7, 8):
        await_slot(slot, own=False)

    share = pltpu.make_async_remote_copy(
        CB.at[:, 16:16 + CROWS, :], CN.at[:, 16:16 + CROWS, :], send_share, recv_share, (jnp.maximum(me - 1, 0), row, col), MESH)

    @pl.when(core == 1)
    def _():
        def put(ref):
            def store(t, w, x):
                ref[t, w] = x
            return store

        unpack(7, put(C12))
        unpack(8, put(S12))

        @pl.when(me == last)
        def _():
            for w in range(2):
                E[0, w, 16:16 + CROWS, :] = NAT[0, w, 8:8 + CROWS, :]

        @pl.when(me != last)
        def _():
            coarse_copies(0, 0, me, send3.at[0])[0].wait_recv()

        await_slot(0, own=False)
        unpack(0, put(V12))

        def advance(slot):
            await_slot(slot)
            heun(V12, A12, C12, S12, T_CHAIN, 2, in_lanes, chain_rows)

            def add(t, w, x):
                V12[t, w] = V12[t, w] + x

            unpack(slot, add)

        def natural(ref):
            for t in range(T_CHAIN):
                for w in range(2):
                    ref[w, pl.ds(t, 8, stride=T_CHAIN), :] = V12[t, w]

        def body(slot, carry):
            @pl.when(slot == me - 1)
            def _():
                natural(CB)
                share.start()

            advance(slot)
            return carry

        lax.fori_loop(1, me, body, 0)
        natural(CN)

        @pl.when(me > 1)
        def _():
            share.wait_send()

    relaxed_copy.wait_recv()

    def relaxed_four(t, w):
        def at(tt, ww):
            return RX[ww, pl.ds(tt, 8, stride=16), :]
        return 0.25 * ((at(2 * t, 2 * w) + at(2 * t, 2 * w + 1)) + (at(2 * t + 1, 2 * w) + at(2 * t + 1, 2 * w + 1)))

    @pl.when(jnp.logical_and(core == 0, me > 0))
    def _():
        share.wait_recv()

    @pl.when(me == 0)
    def _():
        for t in range(8):
            for w in range(2):
                CN[w, pl.ds(16 + t, 8, stride=8), :] = relaxed_four(t, w)

    for t in range(8):
        for w in range(2):
            change = CN[w, pl.ds(16 + t, 8, stride=8), :] - relaxed_four(t, w)
            for tt in (2 * t, 2 * t + 1):
                for ww in (2 * w, 2 * w + 1):
                    Y[ww, pl.ds(tt, 8, stride=16), :] = RX[ww, pl.ds(tt, 8, stride=16), :] + change

    corrected = jnp.concatenate([Y[w, 0:ROWS, :] for w in range(4)], axis=1)
    OUT[...] = move_columns(corrected, GATHER[...])
    store = pltpu.make_async_copy(OUT, out.at[0], store_sem)
    store.start()

    for field in range(3):
        for side in range(2):
            row_copy(field, conduct, side).wait_send()
    for copy in column_copies():
        copy.wait_send()
    for k in (1, 2):
        for copy in coarse_copies(k, 6 + k, me, send_coef.at[k - 1])[1:]:
            copy.wait_send()
    relaxed_copy.wait_send()
    each_receiver(lambda copy: copy.wait_send())
    store.wait()


def local(initial, guesses, conduct, source):
    nt = lax.axis_size("tm")
    f32, bf16 = jnp.float32, jnp.bfloat16
    vmem, dma = pltpu.VMEM, pltpu.SemaphoreType.DMA
    fine, coarse, chain = (T_FINE, 4, 8, 128), (T_COARSE, 2, 8, 128), (T_CHAIN, 2, 8, 128)
    scratch = [
        vmem((3, EXT, 512), f32),
        vmem((4, EXT, 128), f32),
        vmem((2, 2, 3, 8, 128), f32),
        vmem((8, 3, 8, 128), f32),
        vmem(fine, f32),
        vmem(fine, f32),
        vmem(fine, f32),
        vmem(fine, f32),
        vmem((512, 512), bf16),
        vmem((512, COLS), bf16),
        vmem((4, EXT, 128), f32),
        vmem((4, ROWS, 128), f32),
        vmem(coarse, f32),
        vmem(coarse, f32),
        vmem(coarse, f32),
        vmem(coarse, f32),
        vmem((3, 2, EXT // 2, 128), f32),
        vmem((3, 2, 8, 128), f32),
        vmem((9, 2, CROWS + 32, 128), f32),
        vmem((9, 9, 8, 128), f32),
        vmem(chain, f32),
        vmem(chain, f32),
        vmem(chain, f32),
        vmem(chain, f32),
        vmem((2, CROWS + 32, 128), f32),
        vmem((2, CROWS + 32, 128), f32),
        vmem((ROWS, COLS), f32),
        dma((3,)), dma, dma((12,)), dma((12,)), dma, dma, dma((nt // 2, 9)), dma((9, 9)), dma((2, 9)), dma, dma,
        pltpu.SemaphoreType.REGULAR,
    ]
    return pl.pallas_call(
        kernel,
        out_shape=jax.ShapeDtypeStruct(guesses.shape, f32),
        in_specs=[pl.BlockSpec(memory_space=pl.ANY)] * 4,
        out_specs=pl.BlockSpec(memory_space=pl.ANY),
        scratch_shapes=scratch,
        compiler_params=pltpu.CompilerParams(collective_id=0, has_side_effects=True, vmem_limit_bytes=32 * 1024 * 1024),
    )(initial, guesses, conduct, source)


def solution(mesh):
    in_specs = (P("sx", "sy"), P("tm", "sx", "sy"), P("sx", "sy"), P("sx", "sy"))
    out_specs = P("tm", "sx", "sy")
    return jax.shard_map(local, mesh=mesh, in_specs=in_specs, out_specs=out_specs, check_vma=False)
```

```python
import jax
import jax.numpy as jnp
from jax import lax
from jax.experimental import pallas as pl
from jax.experimental.pallas import tpu as pltpu
from jax.sharding import PartitionSpec as P

MESH = pl.DeviceIdType.MESH
FINE = 4
TIME_STEP = 0.035

ROWS, COLS, HALO = 128, 384, 16
EXT = ROWS + 2 * HALO
T_FINE = EXT // 8
T_COARSE = T_FINE // 2
CROWS = ROWS // 2
T_CHAIN = (CROWS + 32) // 8
LOW, HIGH = 16, 112
OWN, FROM_N, FROM_S, FROM_L, FROM_R, FROM_NL, FROM_NR, FROM_SL, FROM_SR, SLOT = 0, 12, 15, 18, 19, 20, 21, 22, 23, 24
R_N, R_S, R_L, R_R, R_NL, R_NR, R_SL, R_SR, R_ALL = 0, 18, 36, 48, 60, 63, 66, 69, 72


def roll(x, shift, axis):
    shift = shift % x.shape[axis]
    return pltpu.roll(x, shift, axis) if shift else x


def flux_pass(src, coef, drift, T, W, emit):
    def load(t):
        values = [src[t, w] for w in range(W)]
        return values, [coef[t, w] * (2.0 + jnp.tanh(values[w])) for w in range(W)]

    def flux(v, k, vn, kn):
        return (k + kn) * (vn - v)

    first, last = load(0), load(T - 1)
    final = [flux(last[0][w], last[1][w], roll(first[0][w], -1, 0), roll(first[1][w], -1, 0)) for w in range(W)]
    above = [roll(f, 1, 0) for f in final]
    here = first
    for t in range(T):
        v, k = here
        if t < T - 1:
            following = last if t + 1 == T - 1 else load(t + 1)
            below = [flux(v[w], k[w], following[0][w], following[1][w]) for w in range(W)]
        else:
            following, below = None, final
        east = [flux(v[w], k[w], v[w + 1], k[w + 1]) for w in range(W - 1)]
        east.append(flux(v[W - 1], k[W - 1], roll(v[0], -1, 1), roll(k[0], -1, 1)))
        west = [roll(east[W - 1], 1, 1)] + east[:-1]
        for w in range(W):
            total = (v[w] + drift[t, w]) + ((east[w] - west[w]) + (below[w] - above[w]))
            emit(t, w, v[w], total)
        here, above = following, below


def heun(state, section, coef, drift, T, W, lanes, row_masks, emit=None):
    def keep(t, w, x):
        if w in (0, W - 1):
            x = x * lanes
        if t in row_masks:
            x = x * row_masks[t]
        return x

    def first(t, w, value, total):
        section[t, w] = keep(t, w, total)

    def second(t, w, value, total):
        result = keep(t, w, 0.5 * (state[t, w] + total))
        if emit is None:
            state[t, w] = result
        else:
            emit(t, w, result)

    flux_pass(state, coef, drift, T, W, first)
    flux_pass(section, coef, drift, T, W, second)


def pieces(x):
    top = x.astype(jnp.bfloat16)
    rest = x - top.astype(jnp.float32)
    middle = rest.astype(jnp.bfloat16)
    low = (rest - middle.astype(jnp.float32)).astype(jnp.bfloat16)
    return top, middle, low


def move_columns(x, choice):
    top, middle, low = [jnp.dot(part, choice, preferred_element_type=jnp.float32) for part in pieces(x)]
    return (top + middle) + low


def pack_group(x, own):
    return [jnp.where(own, x[k], roll(x[3], 96 - 32 * k, 1)) for k in range(3)]


def unpack_group(y, lane):
    parts = [roll(y[k], 32 * k - 96, 1) for k in range(3)]
    return list(y) + [jnp.where(lane < LOW + 32, parts[0], jnp.where(lane < LOW + 64, parts[1], parts[2]))]


def kernel(
    initial, guesses, conduct, source, out,
    X, Y, SR, SC, R1, V, A, CH, SD, SPREAD, GATHER, PROLONG, RN, RS, RX, RR, BASE, RV, CA, CC, CSD, NAT, SB, EB, NB,
    V12, A12, C12, S12, CN, CB, OUT,
    load_sem, store_sem, send1, recv1, send_relaxed, recv_relaxed, send3, recv3, send_coef, send_share, recv_share, ready,
):
    nt, nx, ny = lax.axis_size("tm"), lax.axis_size("sx"), lax.axis_size("sy")
    me, row, col = lax.axis_index("tm"), lax.axis_index("sx"), lax.axis_index("sy")
    chip, core = me // 2, lax.rem(me, 2)
    chips, last = nt // 2, nt - 1
    north, south = lax.rem(row + nx - 1, nx), lax.rem(row + 1, nx)
    left, right = lax.rem(col + ny - 1, ny), lax.rem(col + 1, ny)
    spatial = [(north, col), (south, col), (row, left), (row, right),
               (north, left), (north, right), (south, left), (south, right)]

    barrier = pltpu.get_barrier_semaphore()
    for r, c in spatial:
        pl.semaphore_signal(barrier, inc=1, device_id=(me, r, c), device_id_type=MESH)
    for step in range(1, nt):
        pl.semaphore_signal(barrier, inc=1, device_id=(lax.rem(me + step, nt), row, col), device_id_type=MESH)

    @pl.when(me == last)
    def _():
        pltpu.make_async_copy(initial, X.at[0], load_sem).start()

    @pl.when(me != last)
    def _():
        pltpu.make_async_copy(guesses.at[0], X.at[0], load_sem).start()

    pltpu.make_async_copy(conduct, X.at[1], load_sem).start()
    pltpu.make_async_copy(source, X.at[2], load_sem).start()

    lane = lax.broadcasted_iota(jnp.int32, (8, 128), 1)
    sublane = lax.broadcasted_iota(jnp.int32, (8, 128), 0)
    one, zero = jnp.ones((8, 128), jnp.float32), jnp.zeros((8, 128), jnp.float32)
    own_lanes = jnp.logical_and(lane >= LOW, lane < HIGH)
    at_top, at_bottom, at_left, at_right = row == 0, row == nx - 1, col == 0, col == ny - 1
    in_lanes = jnp.where(jnp.logical_or(jnp.logical_and(lane < LOW, at_left), jnp.logical_and(lane >= HIGH, at_right)), zero, one)

    def strip_mask(which, edge):
        return jnp.where(jnp.logical_and(sublane == which, edge), zero, one)

    def fill(ref, rows, columns):
        ref[...] = jnp.where(rows == columns, 1.0, 0.0).astype(jnp.bfloat16)

    o = lax.broadcasted_iota(jnp.int32, (1, 512), 1)
    fill(SPREAD, lax.broadcasted_iota(jnp.int32, (COLS, 1), 0) + 64, (o & 127) * 4 + (o >> 7))
    o = lax.broadcasted_iota(jnp.int32, (COLS, 1), 0)
    k, l = o >> 7, o & 127
    inside = jnp.logical_and(l >= LOW, l < HIGH)
    packed_from = jnp.where(inside, 4 * l + k, 4 * (((l + 16) & 127) + LOW + 32 * k) + 3)
    fill(GATHER, packed_from, lax.broadcasted_iota(jnp.int32, (1, COLS), 1) + 64)
    o = lax.broadcasted_iota(jnp.int32, (256, 1), 0)
    fill(PROLONG, (o & 127) * 2 + (o >> 7), (lax.broadcasted_iota(jnp.int32, (1, COLS), 1) + 64) >> 1)

    pltpu.make_async_copy(X, X, load_sem).wait()

    for field, factor in ((0, None), (1, 0.25 * TIME_STEP), (2, TIME_STEP)):
        spread = move_columns(X[field], SPREAD[...])
        for w in range(4):
            part = spread[:, 128 * w:128 * w + 128]
            Y[field, w, HALO:HALO + ROWS, :] = part if factor is None else part * factor

    def own_block(field, w, rb):
        return Y[field, w, HALO + 8 * rb:HALO + 8 * rb + 8, :]

    for field in range(3):
        for side in range(2):
            for b in range(2):
                packed = pack_group([own_block(field, w, b if side == 0 else 14 + b) for w in range(4)], own_lanes)
                for k in range(3):
                    SR[side, field * 6 + b * 3 + k] = packed[k]
    eighth = lane // 8
    for field in range(3):
        for side in range(2):
            for quarter in range(4):
                packed = None
                for q in range(16):
                    block = own_block(field, q % 4, 4 * quarter + q // 4)
                    block = roll(block, 8 * q + 100 - LOW if side == 0 else 8 * q - (HIGH - 4), 1)
                    slot_of = (q + 12) % 16 if side == 0 else q
                    packed = block if packed is None else jnp.where(eighth == slot_of, block, packed)
                SC[side, quarter, field] = packed

    pl.semaphore_wait(barrier, 8 + nt - 1)

    first_exchange = [
        pltpu.make_async_remote_copy(s, R1.at[k:k + size], send1, recv1, (me,) + w, MESH)
        for s, k, size, w in [
            (SC.at[1, 3], R_NL, 3, (south, right)),
            (SC.at[0, 3], R_NR, 3, (south, left)),
            (SC.at[1, 0], R_SL, 3, (north, right)),
            (SC.at[0, 0], R_SR, 3, (north, left)),
            (SR.at[0], R_S, 18, (north, col)),
            (SR.at[1], R_N, 18, (south, col)),
        ]
    ]
    for side, k, w in ((1, R_L, (row, right)), (0, R_R, (row, left))):
        for quarter in range(4):
            first_exchange.append(pltpu.make_async_remote_copy(
                SC.at[side, quarter], R1.at[k + 3 * quarter:k + 3 * quarter + 3], send1, recv1, (me,) + w, MESH))
    for copy in first_exchange:
        copy.start()
    pltpu.make_async_copy(R1, R1, recv1).wait()

    for step in range(1, nt):
        pl.semaphore_signal(ready, inc=1, device_id=(lax.rem(me + step, nt), row, col), device_id_type=MESH)

    top16, bottom16 = strip_mask(0, at_top), strip_mask(7, at_bottom)
    masks = [in_lanes * (top16 if t < HALO else 1.0) * (bottom16 if t >= T_FINE - HALO else 1.0) for t in range(T_FINE)]
    odd_slot = (lane & 4) != 0
    for field, dest in ((1, CH), (0, V), (2, SD)):
        halo = {}
        for e in range(EXT // 8):
            if e < 2:
                l, r, rb = R_NL, R_NR, 14 + e
            elif e >= 18:
                l, r, rb = R_SL, R_SR, e - 18
            else:
                rb = e - 2
                l, r = R_L + 3 * (rb // 4), R_R + 3 * (rb // 4)
            if (l, r) not in halo:
                halo[l, r] = jnp.where(odd_slot, R1[r + field], R1[l + field])
            if e < 2 or e >= 18:
                start = (R_N + e * 3 if e < 2 else R_S + (e - 18) * 3) + field * 6
                values = unpack_group([R1[start + k] for k in range(3)], lane)
            else:
                values = [own_block(field, w, rb) for w in range(4)]
            for w in range(4):
                q = (rb % 4) * 4 + w
                Y[field, w, 8 * e:8 * e + 8, :] = jnp.where(own_lanes, values[w], roll(halo[l, r], LOW - 4 - 8 * q, 1))
        for t in range(T_FINE):
            for w in range(4):
                dest[t, w] = Y[field, w, pl.ds(t, 8, stride=T_FINE), :] * masks[t]

    def four(ref, t, w):
        return (ref[2 * t, 2 * w] + ref[2 * t, 2 * w + 1]) + (ref[2 * t + 1, 2 * w] + ref[2 * t + 1, 2 * w + 1])

    def pack_coarse(which):
        def block(rb, w):
            return NAT[which, w, 8 + 8 * rb:16 + 8 * rb, :]

        for g in range(4):
            packed = pack_group([block(2 * g + i // 2, i % 2) for i in range(4)], own_lanes)
            for k in range(3):
                SB[which, 3 * g + k] = packed[k]
        for side in range(2):
            packed = None
            for q in range(16):
                moved = roll(block(q // 2, q % 2), 8 * q - LOW if side == 0 else 8 * q - (HIGH - 8), 1)
                packed = moved if packed is None else jnp.where(eighth == q, moved, packed)
            SB[which, 12 + side] = packed

    def coarse_copies(which, slot, tm, send, recv):
        src = SB.at[which]
        plan = [
            (12, 1, FROM_SR, (north, left)),
            (13, 1, FROM_SL, (north, right)),
            (12, 1, FROM_NR, (south, left)),
            (13, 1, FROM_NL, (south, right)),
            (0, 3, FROM_S, (north, col)),
            (9, 3, FROM_N, (south, col)),
            (12, 1, FROM_R, (row, left)),
            (13, 1, FROM_L, (row, right)),
            (0, 12, OWN, (row, col)),
        ]
        return [pltpu.make_async_remote_copy(src.at[a:a + size], EB.at[slot, k:k + size], send, recv, (tm,) + w, MESH)
                for a, size, k, w in plan]

    for t in range(T_COARSE):
        for w in range(2):
            c, s = 0.25 * four(CH, t, w), four(SD, t, w)
            CC[t, w] = c
            CSD[t, w] = s
            NAT[1, w, pl.ds(t, 8, stride=T_COARSE), :] = c
            NAT[2, w, pl.ds(t, 8, stride=T_COARSE), :] = s

    coef_copies = [copy for k in (1, 2) for copy in coarse_copies(k, 6 + k, me, send_coef, recv3.at[7])[:8]]

    @pl.when(core == 1)
    def _():
        for k in (1, 2):
            pack_coarse(k)
        for copy in coef_copies:
            copy.start()
        for k in (1, 2):
            for v in range(12):
                EB[6 + k, v] = SB[k, v]

    fine_rows = {HALO - 1: top16, T_FINE - HALO: bottom16}

    def fine_run():
        def body(i, carry):
            heun(V, A, CH, SD, T_FINE, 4, in_lanes, fine_rows)
            return carry

        lax.fori_loop(0, FINE, body, 0)

    fine_run()

    for t in range(T_FINE):
        for w in range(4):
            RN[w, pl.ds(t, 8, stride=T_FINE), :] = V[t, w]
    for rb in range(16):
        packed = pack_group([RN[w, HALO + 8 * rb:HALO + 8 * rb + 8, :] for w in range(4)], own_lanes)
        for k in range(3):
            RS[k, 8 * rb:8 * rb + 8, :] = packed[k]
    relaxed_copy = pltpu.make_async_remote_copy(
        RS, RX, send_relaxed, recv_relaxed, (lax.rem(me + 1, nt), row, col), MESH)
    relaxed_copy.start()
    for t in range(T_COARSE):
        for w in range(2):
            RV[t, w] = 0.25 * four(V, t, w)

    fine_run()

    share_of_psi = jnp.where(me == last, 0.0, 1.0)

    def target(t, w, result):
        NAT[0, w, pl.ds(t, 8, stride=T_COARSE), :] = 0.25 * four(V, t, w) - share_of_psi * result

    coarse_rows = {HALO // 2 - 1: top16, T_COARSE - HALO // 2: bottom16}
    heun(RV, CA, CC, CSD, T_COARSE, 2, in_lanes, coarse_rows, target)
    pack_coarse(0)
    pl.semaphore_wait(ready, nt - 1)

    slot_out = jnp.where(me == last, 0, me + 1)
    is_last = me == last

    def each_receiver(action):
        for k in (2, 3, 1, 0):
            copies = coarse_copies(0, slot_out, 2 * lax.rem(chip + k, chips) + 1, send3.at[k], recv3.at[slot_out])
            if k == 0:
                @pl.when(is_last)
                def _():
                    action(k, copies[:8])
                continue
            reached = jnp.logical_or(is_last, jnp.logical_and(chip + k < chips, me < last - 1))
            tile_only = k == 1

            @pl.when(reached)
            def _():
                if tile_only:
                    @pl.when(core == 0)
                    def _():
                        action(k, copies)

                    @pl.when(core == 1)
                    def _():
                        action(k, copies[8:])
                else:
                    action(k, copies)

    def start(k, copies):
        for copy in copies:
            copy.start()

    def finish(k, copies):
        size = {8: 12, 9: 24, 1: 12}[len(copies)]
        whole = EB.at[0, 0:size]
        pltpu.make_async_copy(whole, whole, send3.at[k]).wait()

    each_receiver(start)

    def unpack(slot, store):
        def halo_at(e):
            if e < 2:
                return EB[slot, FROM_NL], EB[slot, FROM_NR], 6 + e
            if e >= 10:
                return EB[slot, FROM_SL], EB[slot, FROM_SR], e - 10
            return EB[slot, FROM_L], EB[slot, FROM_R], e - 2

        for g in range(6):
            base = FROM_N if g == 0 else FROM_S if g == 5 else OWN + 3 * (g - 1)
            values = unpack_group([EB[slot, base + k] for k in range(3)], lane)
            mask = in_lanes
            if g == 0:
                mask = mask * jnp.where(at_top, 0.0, 1.0)
            if g == 5:
                mask = mask * jnp.where(at_bottom, 0.0, 1.0)
            for i in range(4):
                e, w = 2 * g + i // 2, i % 2
                from_left, from_right, rb = halo_at(e)
                q = rb * 2 + w
                value = jnp.where(lane < LOW, roll(from_left, LOW - 8 - 8 * q, 1), values[i])
                value = jnp.where(lane >= HIGH, roll(from_right, HIGH - 8 * q, 1), value)
                NB[w, 8 * e:8 * e + 8, :] = value * mask
        for t in range(T_CHAIN):
            for w in range(2):
                store(t, w, NB[w, pl.ds(t, 8, stride=T_CHAIN), :])

    def await_vectors(ref, sem):
        pltpu.make_async_copy(ref, ref, sem).wait()

    chain_rows = {15 % T_CHAIN: strip_mask(15 // T_CHAIN, at_top), 80 % T_CHAIN: strip_mask(80 // T_CHAIN, at_bottom)}
    share = pltpu.make_async_remote_copy(
        CB, CN, send_share, recv_share, (jnp.maximum(me - 1, 0), row, col), MESH)

    def natural(ref):
        for t in range(T_CHAIN):
            for w in range(2):
                NB[w, pl.ds(t, 8, stride=T_CHAIN), :] = V12[t, w]
        for w in range(2):
            ref[w] = NB[w, 16:16 + CROWS, :]

    def relaxed_base():
        await_vectors(RX, recv_relaxed)
        for rb in range(16):
            values = unpack_group([RX[k, 8 * rb:8 * rb + 8, :] for k in range(3)], lane)
            for w in range(4):
                RN[w, 8 * rb:8 * rb + 8, :] = values[w]
        for t in range(8):
            for w in range(2):
                def at(tt, ww):
                    return RN[ww, pl.ds(tt, 8, stride=16), :]
                RR[t, w] = 0.25 * ((at(2 * t, 2 * w) + at(2 * t, 2 * w + 1)) + (at(2 * t + 1, 2 * w) + at(2 * t + 1, 2 * w + 1)))
        base = move_columns(jnp.concatenate([RX[k] for k in range(3)], axis=1), GATHER[...])
        for k in range(3):
            BASE[k] = base[:, 128 * k:128 * k + 128]

    @pl.when(core == 1)
    def _():
        def put(ref):
            def store(t, w, x):
                ref[t, w] = x
            return store

        await_vectors(EB.at[7:9, FROM_N:SLOT], recv3.at[7])
        unpack(7, put(C12))
        unpack(8, put(S12))

    relaxed_base()

    @pl.when(core == 1)
    def _():
        def put(t, w, x):
            V12[t, w] = x

        def add(t, w, x):
            V12[t, w] = V12[t, w] + x

        @pl.when(is_last)
        def _():
            for v in range(12):
                EB[0, v] = SB[0, v]
            await_vectors(EB.at[0, FROM_N:SLOT], recv3.at[0])

        @pl.when(me == 1)
        def _():
            await_vectors(EB.at[0, 0:FROM_N], recv3.at[0])

        @pl.when(jnp.logical_and(me != last, me > 1))
        def _():
            await_vectors(EB.at[0], recv3.at[0])

        unpack(0, put)

        def body(slot, carry):
            final = slot == me - 1

            @pl.when(final)
            def _():
                natural(CB)
                share.start()
                await_vectors(EB.at[slot, 0:FROM_N], recv3.at[slot])

            @pl.when(jnp.logical_not(final))
            def _():
                await_vectors(EB.at[slot], recv3.at[slot])

            heun(V12, A12, C12, S12, T_CHAIN, 2, in_lanes, chain_rows)
            unpack(slot, add)
            return carry

        lax.fori_loop(1, me, body, 0)
        natural(CN)

        @pl.when(me > 1)
        def _():
            share.wait_send()

    @pl.when(jnp.logical_and(core == 0, me > 0))
    def _():
        share.wait_recv()

    @pl.when(me == 0)
    def _():
        for t in range(8):
            for w in range(2):
                CN[w, pl.ds(t, 8, stride=8), :] = RR[t, w]

    change = jnp.concatenate(
        [jnp.concatenate([jnp.where(own_lanes, CN[w, pl.ds(t, 8, stride=8), :] - RR[t, w], 0.0) for w in range(2)], axis=1)
         for t in range(8)], axis=0)
    change = move_columns(change, PROLONG[...])
    for t in range(8):
        for k in range(3):
            for tt in (2 * t, 2 * t + 1):
                OUT[k, pl.ds(tt, 8, stride=16), :] = (
                    BASE[k, pl.ds(tt, 8, stride=16), :] + change[8 * t:8 * t + 8, 128 * k:128 * k + 128])
    for k in range(3):
        pltpu.make_async_copy(OUT.at[k], out.at[0, :, 128 * k:128 * k + 128], store_sem).start()

    await_vectors(R1, send1)

    @pl.when(core == 1)
    def _():
        await_vectors(EB.at[7:9, FROM_N:SLOT], send_coef)

    relaxed_copy.wait_send()
    each_receiver(finish)
    await_vectors(OUT, store_sem)


def local(initial, guesses, conduct, source):
    nt = lax.axis_size("tm")
    f32, bf16 = jnp.float32, jnp.bfloat16
    vmem, dma = pltpu.VMEM, pltpu.SemaphoreType.DMA
    fine, coarse, chain = (T_FINE, 4, 8, 128), (T_COARSE, 2, 8, 128), (T_CHAIN, 2, 8, 128)
    scratch = [
        vmem((3, ROWS, COLS), f32),
        vmem((3, 4, EXT, 128), f32),
        vmem((2, 18, 8, 128), f32),
        vmem((2, 4, 3, 8, 128), f32),
        vmem((R_ALL, 8, 128), f32),
        vmem(fine, f32),
        vmem(fine, f32),
        vmem(fine, f32),
        vmem(fine, f32),
        vmem((COLS, 512), bf16),
        vmem((COLS, COLS), bf16),
        vmem((256, COLS), bf16),
        vmem((4, EXT, 128), f32),
        vmem((3, ROWS, 128), f32),
        vmem((3, ROWS, 128), f32),
        vmem((8, 2, 8, 128), f32),
        vmem((3, ROWS, 128), f32),
        vmem(coarse, f32),
        vmem(coarse, f32),
        vmem(coarse, f32),
        vmem(coarse, f32),
        vmem((3, 2, EXT // 2, 128), f32),
        vmem((3, 14, 8, 128), f32),
        vmem((9, SLOT, 8, 128), f32),
        vmem((2, CROWS + 32, 128), f32),
        vmem(chain, f32),
        vmem(chain, f32),
        vmem(chain, f32),
        vmem(chain, f32),
        vmem((2, CROWS, 128), f32),
        vmem((2, CROWS, 128), f32),
        vmem((3, ROWS, 128), f32),
        dma, dma, dma, dma, dma, dma, dma((nt // 2,)), dma((8,)), dma, dma, dma,
        pltpu.SemaphoreType.REGULAR,
    ]
    return pl.pallas_call(
        kernel,
        out_shape=jax.ShapeDtypeStruct(guesses.shape, f32),
        in_specs=[pl.BlockSpec(memory_space=pl.ANY)] * 4,
        out_specs=pl.BlockSpec(memory_space=pl.ANY),
        scratch_shapes=scratch,
        compiler_params=pltpu.CompilerParams(collective_id=0, has_side_effects=True, vmem_limit_bytes=60 * 1024 * 1024),
    )(initial, guesses, conduct, source)


def solution(mesh):
    in_specs = (P("sx", "sy"), P("tm", "sx", "sy"), P("sx", "sy"), P("sx", "sy"))
    out_specs = P("tm", "sx", "sy")
    return jax.shard_map(local, mesh=mesh, in_specs=in_specs, out_specs=out_specs, check_vma=False)
```

```python
import jax
import jax.numpy as jnp
from jax import lax
from jax.experimental import pallas as pl
from jax.experimental.pallas import tpu as pltpu
from jax.sharding import PartitionSpec as P

MESH = pl.DeviceIdType.MESH
FINE = 4
TIME_STEP = 0.035

ROWS, COLS, HALO = 128, 384, 16
EXT = ROWS + 2 * HALO
T_FINE = EXT // 8
T_COARSE = T_FINE // 2
CROWS = ROWS // 2
T_CHAIN = (CROWS + 32) // 8
LOW, HIGH = 16, 112
OWN, FROM_N, FROM_S, FROM_L, FROM_R, SLOT = 0, 12, 15, 18, 19, 21
FROM_NL, FROM_NR, FROM_SL, FROM_SR = range(4)
R_N, R_S, R_L, R_R, R_NL, R_NR, R_SL, R_SR, R_ALL = 0, 18, 36, 48, 60, 61, 62, 63, 64


def roll(x, shift, axis):
    shift = shift % x.shape[axis]
    return pltpu.roll(x, shift, axis) if shift else x


def flux_pass(src, coef, drift, T, W, emit):
    def load(t):
        values = [src[t, w] for w in range(W)]
        return values, [coef[t, w] * (2.0 + jnp.tanh(values[w])) for w in range(W)]

    def flux(v, k, vn, kn):
        return (k + kn) * (vn - v)

    first, last = load(0), load(T - 1)
    final = [flux(last[0][w], last[1][w], roll(first[0][w], -1, 0), roll(first[1][w], -1, 0)) for w in range(W)]
    above = [roll(f, 1, 0) for f in final]
    here = first
    for t in range(T):
        v, k = here
        if t < T - 1:
            following = last if t + 1 == T - 1 else load(t + 1)
            below = [flux(v[w], k[w], following[0][w], following[1][w]) for w in range(W)]
        else:
            following, below = None, final
        east = [flux(v[w], k[w], v[w + 1], k[w + 1]) for w in range(W - 1)]
        east.append(flux(v[W - 1], k[W - 1], roll(v[0], -1, 1), roll(k[0], -1, 1)))
        west = [roll(east[W - 1], 1, 1)] + east[:-1]
        for w in range(W):
            emit(t, w, v[w], drift[t, w] + ((east[w] - west[w]) + (below[w] - above[w])))
        here, above = following, below


def heun(state, section, coef, drift, T, W, lanes, row_masks, emit=None):
    def keep(t, w, x):
        if w in (0, W - 1):
            x = x * lanes
        if t in row_masks:
            x = x * row_masks[t]
        return x

    def first(t, w, value, increment):
        middle = value + increment
        state[t, w] = middle
        section[t, w] = keep(t, w, middle + increment)

    def second(t, w, value, increment):
        result = keep(t, w, state[t, w] + increment)
        if emit is None:
            state[t, w] = result
        else:
            emit(t, w, result)

    flux_pass(state, coef, drift, T, W, first)
    flux_pass(section, coef, drift, T, W, second)


def pieces(x):
    top = x.astype(jnp.bfloat16)
    rest = x - top.astype(jnp.float32)
    middle = rest.astype(jnp.bfloat16)
    low = (rest - middle.astype(jnp.float32)).astype(jnp.bfloat16)
    return top, middle, low


def move_columns(x, choice):
    top, middle, low = [jnp.dot(part, choice, preferred_element_type=jnp.float32) for part in pieces(x)]
    return (top + middle) + low


def skew(x, step, sublane):
    moved = [roll(x, step * k, 1) for k in range(4)]
    i = sublane & 3
    return jnp.where(i < 2, jnp.where(i == 0, moved[0], moved[1]), jnp.where(i == 2, moved[2], moved[3]))


def pack_group(x, own):
    return [jnp.where(own, x[k], roll(x[3], 96 - 32 * k, 1)) for k in range(3)]


def unpack_group(y, lane):
    parts = [roll(y[k], 32 * k - 96, 1) for k in range(3)]
    return list(y) + [jnp.where(lane < LOW + 32, parts[0], jnp.where(lane < LOW + 64, parts[1], parts[2]))]


def kernel(
    initial, guesses, conduct, source, out,
    X, Y, SR, SC, SK, R1, V, A, CH, SD, SPREAD, GATHER, PROLONG, RN, RS, RX, RR, BASE, RV, CA, CC, CSD, NAT, SB, SE, EB, EE, NB,
    V12, A12, C12, S12, CN, CB, OUT,
    load_sem, store_sem, send1, recv1, send_relaxed, recv_relaxed, send3, recv3, send_coef, send_share, recv_share, ready,
):
    nt, nx, ny = lax.axis_size("tm"), lax.axis_size("sx"), lax.axis_size("sy")
    me, row, col = lax.axis_index("tm"), lax.axis_index("sx"), lax.axis_index("sy")
    chip, core = me // 2, lax.rem(me, 2)
    chips, last = nt // 2, nt - 1
    north, south = lax.rem(row + nx - 1, nx), lax.rem(row + 1, nx)
    left, right = lax.rem(col + ny - 1, ny), lax.rem(col + 1, ny)
    spatial = [(north, col), (south, col), (row, left), (row, right),
               (north, left), (north, right), (south, left), (south, right)]

    barrier = pltpu.get_barrier_semaphore()
    for r, c in spatial:
        pl.semaphore_signal(barrier, inc=1, device_id=(me, r, c), device_id_type=MESH)
    for step in range(1, nt):
        pl.semaphore_signal(barrier, inc=1, device_id=(lax.rem(me + step, nt), row, col), device_id_type=MESH)

    def await_vectors(ref, sem):
        pltpu.make_async_copy(ref, ref, sem).wait()

    @pl.when(me == last)
    def _():
        pltpu.make_async_copy(initial, X.at[0], load_sem).start()

    @pl.when(me != last)
    def _():
        pltpu.make_async_copy(guesses.at[0], X.at[0], load_sem).start()

    pltpu.make_async_copy(conduct, X.at[1], load_sem).start()
    pltpu.make_async_copy(source, X.at[2], load_sem).start()

    lane = lax.broadcasted_iota(jnp.int32, (8, 128), 1)
    sublane = lax.broadcasted_iota(jnp.int32, (8, 128), 0)
    one, zero = jnp.ones((8, 128), jnp.float32), jnp.zeros((8, 128), jnp.float32)
    own_lanes = jnp.logical_and(lane >= LOW, lane < HIGH)
    at_top, at_bottom, at_left, at_right = row == 0, row == nx - 1, col == 0, col == ny - 1
    in_lanes = jnp.where(jnp.logical_or(jnp.logical_and(lane < LOW, at_left), jnp.logical_and(lane >= HIGH, at_right)), zero, one)

    def strip_mask(which, edge):
        return jnp.where(jnp.logical_and(sublane == which, edge), zero, one)

    def fill(ref, rows, columns):
        ref[...] = jnp.where(rows == columns, 1.0, 0.0).astype(jnp.bfloat16)

    o = lax.broadcasted_iota(jnp.int32, (1, 512), 1)
    fill(SPREAD, lax.broadcasted_iota(jnp.int32, (COLS, 1), 0) + 64, (o & 127) * 4 + (o >> 7))
    o = lax.broadcasted_iota(jnp.int32, (COLS, 1), 0)
    k, l = o >> 7, o & 127
    inside = jnp.logical_and(l >= LOW, l < HIGH)
    packed_from = jnp.where(inside, 4 * l + k, 4 * (((l + 16) & 127) + LOW + 32 * k) + 3)
    fill(GATHER, packed_from, lax.broadcasted_iota(jnp.int32, (1, COLS), 1) + 64)
    o = lax.broadcasted_iota(jnp.int32, (256, 1), 0)
    fill(PROLONG, (o & 127) * 2 + (o >> 7), (lax.broadcasted_iota(jnp.int32, (1, COLS), 1) + 64) >> 1)

    pltpu.make_async_copy(X, X, load_sem).wait()

    for field, factor in ((0, None), (1, 0.125 * TIME_STEP), (2, 0.5 * TIME_STEP)):
        spread = move_columns(X[field], SPREAD[...])
        for w in range(4):
            part = spread[:, 128 * w:128 * w + 128]
            Y[field, w, HALO:HALO + ROWS, :] = part if factor is None else part * factor

    def own_block(field, w, rb):
        return Y[field, w, HALO + 8 * rb:HALO + 8 * rb + 8, :]

    for field in range(3):
        for side in range(2):
            for b in range(2):
                packed = pack_group([own_block(field, w, b if side == 0 else 14 + b) for w in range(4)], own_lanes)
                for k in range(3):
                    SR[side, field * 6 + b * 3 + k] = packed[k]
    eighth = lane // 8
    for field in range(3):
        for side in range(2):
            for quarter in range(4):
                packed = None
                for q in range(16):
                    block = own_block(field, q % 4, 4 * quarter + q // 4)
                    block = roll(block, 8 * q + 100 - LOW if side == 0 else 8 * q - (HIGH - 4), 1)
                    slot_of = (q + 12) % 16 if side == 0 else q
                    packed = block if packed is None else jnp.where(eighth == slot_of, block, packed)
                SC[side, quarter, field] = packed
    odd_slot = (lane & 4) != 0
    for side in range(2):
        for end, quarter in ((0, 0), (1, 3)):
            fields = [SC[side, quarter, field] for field in range(3)]
            if side == 1:
                half = (lane < 64) if end == 0 else (lane >= 64)
                pair = jnp.where(odd_slot, roll(fields[1], 4, 1), fields[0])
            else:
                half = ((lane + 32) & 127) < 64 if end == 0 else ((lane + 32) & 127) >= 64
                pair = jnp.where(odd_slot, fields[0], roll(fields[1], -4, 1))
            SK[side, end] = jnp.where(half, pair, roll(fields[2], 64, 1))

    def pack_coarse(which):
        def block(rb, w):
            return NAT[which, w, 8 + 8 * rb:16 + 8 * rb, :]

        for g in range(4):
            packed = pack_group([block(2 * g + i // 2, i % 2) for i in range(4)], own_lanes)
            for k in range(3):
                SB[which, 3 * g + k] = packed[k]
        for side in range(2):
            packed = None
            for q in range(16):
                moved = roll(block(q // 2, q % 2), 8 * q - LOW if side == 0 else 8 * q - (HIGH - 8), 1)
                packed = moved if packed is None else jnp.where(eighth == q, moved, packed)
            SB[which, 12 + side] = packed
            for end in range(2):
                moved = skew(roll(packed, 32 if end else 0, 1), 32, sublane)
                moved = jnp.where((lane // 32) == (sublane & 3), moved, 0.0)
                moved = moved + roll(moved, 1, 0)
                moved = moved + roll(moved, 2, 0)
                SE[which, 2 * side + end, 0:1, :] = moved[3:4, :]
                SE[which, 2 * side + end, 1:2, :] = moved[7:8, :]

    def coarse_copies(which, slot, tm, send, recv):
        def copy(src, dst, where):
            return pltpu.make_async_remote_copy(src, dst, send, recv, (tm,) + where, MESH)

        def vectors(a, size, k, where):
            return copy(SB.at[which, a:a + size], EB.at[slot, k:k + size], where)

        return [
            copy(SE.at[which, 0], EE.at[slot, FROM_SR], (north, left)),
            copy(SE.at[which, 2], EE.at[slot, FROM_SL], (north, right)),
            copy(SE.at[which, 1], EE.at[slot, FROM_NR], (south, left)),
            copy(SE.at[which, 3], EE.at[slot, FROM_NL], (south, right)),
            vectors(0, 3, FROM_S, (north, col)),
            vectors(9, 3, FROM_N, (south, col)),
            vectors(12, 1, FROM_R, (row, left)),
            vectors(13, 1, FROM_L, (row, right)),
            vectors(0, 12, OWN, (row, col)),
        ]

    coef_copies = [copy for k in (1, 2) for copy in coarse_copies(k, 6 + k, me, send_coef, recv3.at[7])[:8]]

    @pl.when(core == 1)
    def _():
        for k in (1, 2):
            for rb in range(8):
                for w in range(2):
                    def at(ww, r):
                        return Y[k, ww, pl.ds(HALO + 16 * rb + r, 8, stride=2), :]
                    total = (at(2 * w, 0) + at(2 * w + 1, 0)) + (at(2 * w, 1) + at(2 * w + 1, 1))
                    NAT[k, w, 8 + 8 * rb:16 + 8 * rb, :] = 0.25 * total if k == 1 else total
            pack_coarse(k)
            for v in range(12):
                EB[6 + k, v] = SB[k, v]

    pl.semaphore_wait(barrier, 8 + nt - 1)

    first_exchange = [
        pltpu.make_async_remote_copy(s, R1.at[k:k + size], send1, recv1, (me,) + w, MESH)
        for s, k, size, w in [
            (SK.at[1, 1:2], R_NL, 1, (south, right)),
            (SK.at[0, 1:2], R_NR, 1, (south, left)),
            (SK.at[1, 0:1], R_SL, 1, (north, right)),
            (SK.at[0, 0:1], R_SR, 1, (north, left)),
            (SR.at[0], R_S, 18, (north, col)),
            (SR.at[1], R_N, 18, (south, col)),
        ]
    ]
    for side, k, w in ((1, R_L, (row, right)), (0, R_R, (row, left))):
        for quarter in range(4):
            first_exchange.append(pltpu.make_async_remote_copy(
                SC.at[side, quarter], R1.at[k + 3 * quarter:k + 3 * quarter + 3], send1, recv1, (me,) + w, MESH))
    for copy in first_exchange:
        copy.start()

    @pl.when(core == 1)
    def _():
        for copy in coef_copies:
            copy.start()

    pltpu.make_async_copy(R1, R1, recv1).wait()

    for step in range(1, nt):
        pl.semaphore_signal(ready, inc=1, device_id=(lax.rem(me + step, nt), row, col), device_id_type=MESH)

    top16, bottom16 = strip_mask(0, at_top), strip_mask(7, at_bottom)
    masks = [in_lanes * (top16 if t < HALO else 1.0) * (bottom16 if t >= T_FINE - HALO else 1.0) for t in range(T_FINE)]
    for field, dest in ((1, CH), (0, V), (2, SD)):
        halo = {}
        for e in range(EXT // 8):
            if e < 2:
                l, r, rb = R_NL, R_NR, 14 + e
            elif e >= 18:
                l, r, rb = R_SL, R_SR, e - 18
            else:
                rb = e - 2
                l, r = R_L + 3 * (rb // 4), R_R + 3 * (rb // 4)
            if (l, r) not in halo:
                if e < 2 or e >= 18:
                    shift = (0, 4, 64)[field]
                    halo[l, r] = jnp.where(odd_slot, roll(R1[r], shift, 1), roll(R1[l], -shift, 1))
                else:
                    halo[l, r] = jnp.where(odd_slot, R1[r + field], R1[l + field])
            if e < 2 or e >= 18:
                start = (R_N + e * 3 if e < 2 else R_S + (e - 18) * 3) + field * 6
                values = unpack_group([R1[start + k] for k in range(3)], lane)
            else:
                values = [own_block(field, w, rb) for w in range(4)]
            for w in range(4):
                q = (rb % 4) * 4 + w
                Y[field, w, 8 * e:8 * e + 8, :] = jnp.where(own_lanes, values[w], roll(halo[l, r], LOW - 4 - 8 * q, 1))
        for t in range(T_FINE):
            for w in range(4):
                dest[t, w] = Y[field, w, pl.ds(t, 8, stride=T_FINE), :] * masks[t]

    def four(ref, t, w):
        return (ref[2 * t, 2 * w] + ref[2 * t, 2 * w + 1]) + (ref[2 * t + 1, 2 * w] + ref[2 * t + 1, 2 * w + 1])

    for t in range(T_COARSE):
        for w in range(2):
            CC[t, w] = 0.25 * four(CH, t, w)
            CSD[t, w] = four(SD, t, w)

    fine_rows = {HALO - 1: top16, T_FINE - HALO: bottom16}

    def fine_run():
        def body(i, carry):
            heun(V, A, CH, SD, T_FINE, 4, in_lanes, fine_rows)
            return carry

        lax.fori_loop(0, FINE, body, 0)

    fine_run()

    for t in range(T_FINE):
        for w in range(4):
            RN[w, pl.ds(t, 8, stride=T_FINE), :] = V[t, w]
    for rb in range(16):
        packed = pack_group([RN[w, HALO + 8 * rb:HALO + 8 * rb + 8, :] for w in range(4)], own_lanes)
        for k in range(3):
            RS[k, 8 * rb:8 * rb + 8, :] = packed[k]
    relaxed_copy = pltpu.make_async_remote_copy(
        RS, RX, send_relaxed, recv_relaxed, (lax.rem(me + 1, nt), row, col), MESH)
    relaxed_copy.start()
    for t in range(T_COARSE):
        for w in range(2):
            RV[t, w] = 0.25 * four(V, t, w)

    fine_run()

    share_of_psi = jnp.where(me == last, 0.0, 1.0)

    def target(t, w, result):
        NAT[0, w, pl.ds(t, 8, stride=T_COARSE), :] = 0.25 * four(V, t, w) - share_of_psi * result

    coarse_rows = {HALO // 2 - 1: top16, T_COARSE - HALO // 2: bottom16}
    heun(RV, CA, CC, CSD, T_COARSE, 2, in_lanes, coarse_rows, target)
    pack_coarse(0)
    pl.semaphore_wait(ready, nt - 1)

    slot_out = jnp.where(me == last, 0, me + 1)
    is_last = me == last

    def each_receiver(action):
        for k in (2, 3, 1, 0):
            copies = coarse_copies(0, slot_out, 2 * lax.rem(chip + k, chips) + 1, send3.at[k], recv3.at[slot_out])
            if k == 0:
                @pl.when(is_last)
                def _():
                    action(k, copies[:8])
                continue
            reached = jnp.logical_or(is_last, jnp.logical_and(chip + k < chips, me < last - 1))
            tile_only = k == 1

            @pl.when(reached)
            def _():
                if tile_only:
                    @pl.when(core == 0)
                    def _():
                        action(k, copies)

                    @pl.when(core == 1)
                    def _():
                        action(k, copies[8:])
                else:
                    action(k, copies)

    def start(k, copies):
        for copy in copies:
            copy.start()

    def finish(k, copies):
        size = {8: 9, 9: 21, 1: 12}[len(copies)]
        await_vectors(EB.at[0, 0:size], send3.at[k])

    each_receiver(start)

    def unpack(slot, store):
        def halo_at(e):
            if e < 2:
                return corners[FROM_NL], corners[FROM_NR], e
            if e >= 10:
                return corners[FROM_SL], corners[FROM_SR], e - 10
            return EB[slot, FROM_L], EB[slot, FROM_R], e - 2

        corners = []
        for k in range(4):
            two = jnp.where(sublane < 4, EE[slot, k, 0:1, :], EE[slot, k, 1:2, :])
            corners.append(skew(two, -32, sublane))

        for g in range(6):
            base = FROM_N if g == 0 else FROM_S if g == 5 else OWN + 3 * (g - 1)
            values = unpack_group([EB[slot, base + k] for k in range(3)], lane)
            mask = in_lanes
            if g == 0:
                mask = mask * jnp.where(at_top, 0.0, 1.0)
            if g == 5:
                mask = mask * jnp.where(at_bottom, 0.0, 1.0)
            for i in range(4):
                e, w = 2 * g + i // 2, i % 2
                from_left, from_right, rb = halo_at(e)
                q = rb * 2 + w
                value = jnp.where(lane < LOW, roll(from_left, LOW - 8 - 8 * q, 1), values[i])
                value = jnp.where(lane >= HIGH, roll(from_right, HIGH - 8 * q, 1), value)
                NB[w, 8 * e:8 * e + 8, :] = value * mask
        for t in range(T_CHAIN):
            for w in range(2):
                store(t, w, NB[w, pl.ds(t, 8, stride=T_CHAIN), :])

    chain_rows = {15 % T_CHAIN: strip_mask(15 // T_CHAIN, at_top), 80 % T_CHAIN: strip_mask(80 // T_CHAIN, at_bottom)}
    share = pltpu.make_async_remote_copy(
        CB, CN, send_share, recv_share, (jnp.maximum(me - 1, 0), row, col), MESH)

    def natural(ref):
        for t in range(T_CHAIN):
            for w in range(2):
                NB[w, pl.ds(t, 8, stride=T_CHAIN), :] = V12[t, w]
        for w in range(2):
            ref[w] = NB[w, 16:16 + CROWS, :]

    def relaxed_base():
        await_vectors(RX, recv_relaxed)
        for rb in range(16):
            values = unpack_group([RX[k, 8 * rb:8 * rb + 8, :] for k in range(3)], lane)
            for w in range(4):
                RN[w, 8 * rb:8 * rb + 8, :] = values[w]
        for t in range(8):
            for w in range(2):
                def at(tt, ww):
                    return RN[ww, pl.ds(tt, 8, stride=16), :]
                RR[t, w] = 0.25 * ((at(2 * t, 2 * w) + at(2 * t, 2 * w + 1)) + (at(2 * t + 1, 2 * w) + at(2 * t + 1, 2 * w + 1)))
        base = move_columns(jnp.concatenate([RX[k] for k in range(3)], axis=1), GATHER[...])
        for k in range(3):
            BASE[k] = base[:, 128 * k:128 * k + 128]

    @pl.when(core == 1)
    def _():
        def put(ref):
            def store(t, w, x):
                ref[t, w] = x
            return store

        await_vectors(EB.at[7:9, FROM_N:SLOT], recv3.at[7])
        unpack(7, put(C12))
        unpack(8, put(S12))

    relaxed_base()

    @pl.when(core == 1)
    def _():
        def put(t, w, x):
            V12[t, w] = x

        def add(t, w, x):
            V12[t, w] = V12[t, w] + x

        @pl.when(is_last)
        def _():
            for v in range(12):
                EB[0, v] = SB[0, v]
            await_vectors(EB.at[0, FROM_N:SLOT], recv3.at[0])

        @pl.when(me == 1)
        def _():
            await_vectors(EB.at[0, 0:FROM_N], recv3.at[0])

        @pl.when(jnp.logical_and(me != last, me > 1))
        def _():
            await_vectors(EB.at[0], recv3.at[0])

        unpack(0, put)

        def body(slot, carry):
            final = slot == me - 1

            @pl.when(final)
            def _():
                natural(CB)
                share.start()
                await_vectors(EB.at[slot, 0:FROM_N], recv3.at[slot])

            @pl.when(jnp.logical_not(final))
            def _():
                await_vectors(EB.at[slot], recv3.at[slot])

            heun(V12, A12, C12, S12, T_CHAIN, 2, in_lanes, chain_rows)
            unpack(slot, add)
            return carry

        lax.fori_loop(1, me, body, 0)
        natural(CN)

        @pl.when(me > 1)
        def _():
            share.wait_send()

    @pl.when(jnp.logical_and(core == 0, me > 0))
    def _():
        share.wait_recv()

    @pl.when(me == 0)
    def _():
        for t in range(8):
            for w in range(2):
                CN[w, pl.ds(t, 8, stride=8), :] = RR[t, w]

    change = jnp.concatenate(
        [jnp.concatenate([jnp.where(own_lanes, CN[w, pl.ds(t, 8, stride=8), :] - RR[t, w], 0.0) for w in range(2)], axis=1)
         for t in range(8)], axis=0)
    change = move_columns(change, PROLONG[...])
    for t in range(8):
        for k in range(3):
            for tt in (2 * t, 2 * t + 1):
                OUT[k, pl.ds(tt, 8, stride=16), :] = (
                    BASE[k, pl.ds(tt, 8, stride=16), :] + change[8 * t:8 * t + 8, 128 * k:128 * k + 128])
    for k in range(3):
        pltpu.make_async_copy(OUT.at[k], out.at[0, :, 128 * k:128 * k + 128], store_sem).start()

    await_vectors(R1, send1)

    @pl.when(core == 1)
    def _():
        await_vectors(EB.at[7:9, FROM_N:SLOT], send_coef)

    relaxed_copy.wait_send()
    each_receiver(finish)
    await_vectors(OUT, store_sem)


def local(initial, guesses, conduct, source):
    nt = lax.axis_size("tm")
    f32, bf16 = jnp.float32, jnp.bfloat16
    vmem, dma = pltpu.VMEM, pltpu.SemaphoreType.DMA
    fine, coarse, chain = (T_FINE, 4, 8, 128), (T_COARSE, 2, 8, 128), (T_CHAIN, 2, 8, 128)
    scratch = [
        vmem((3, ROWS, COLS), f32),
        vmem((3, 4, EXT, 128), f32),
        vmem((2, 18, 8, 128), f32),
        vmem((2, 4, 3, 8, 128), f32),
        vmem((2, 2, 8, 128), f32),
        vmem((R_ALL, 8, 128), f32),
        vmem(fine, f32),
        vmem(fine, f32),
        vmem(fine, f32),
        vmem(fine, f32),
        vmem((COLS, 512), bf16),
        vmem((COLS, COLS), bf16),
        vmem((256, COLS), bf16),
        vmem((4, EXT, 128), f32),
        vmem((3, ROWS, 128), f32),
        vmem((3, ROWS, 128), f32),
        vmem((8, 2, 8, 128), f32),
        vmem((3, ROWS, 128), f32),
        vmem(coarse, f32),
        vmem(coarse, f32),
        vmem(coarse, f32),
        vmem(coarse, f32),
        vmem((3, 2, EXT // 2, 128), f32),
        vmem((3, 14, 8, 128), f32),
        vmem((3, 4, 2, 128), f32),
        vmem((9, SLOT, 8, 128), f32),
        vmem((9, 4, 2, 128), f32),
        vmem((2, CROWS + 32, 128), f32),
        vmem(chain, f32),
        vmem(chain, f32),
        vmem(chain, f32),
        vmem(chain, f32),
        vmem((2, CROWS, 128), f32),
        vmem((2, CROWS, 128), f32),
        vmem((3, ROWS, 128), f32),
        dma, dma, dma, dma, dma, dma, dma((nt // 2,)), dma((8,)), dma, dma, dma,
        pltpu.SemaphoreType.REGULAR,
    ]
    return pl.pallas_call(
        kernel,
        out_shape=jax.ShapeDtypeStruct(guesses.shape, f32),
        in_specs=[pl.BlockSpec(memory_space=pl.ANY)] * 4,
        out_specs=pl.BlockSpec(memory_space=pl.ANY),
        scratch_shapes=scratch,
        compiler_params=pltpu.CompilerParams(collective_id=0, has_side_effects=True, vmem_limit_bytes=54976 * 1024),
    )(initial, guesses, conduct, source)


def solution(mesh):
    in_specs = (P("sx", "sy"), P("tm", "sx", "sy"), P("sx", "sy"), P("sx", "sy"))
    out_specs = P("tm", "sx", "sy")
    return jax.shard_map(local, mesh=mesh, in_specs=in_specs, out_specs=out_specs, check_vma=False)
```

```python
import jax
import jax.numpy as jnp
from jax import lax
from jax.experimental import pallas as pl
from jax.experimental.pallas import tpu as pltpu
from jax.sharding import PartitionSpec as P

MESH = pl.DeviceIdType.MESH
FINE = 4
TIME_STEP = 0.035

ROWS, COLS, HALO = 128, 384, 16
EXT = ROWS + 2 * HALO
T_FINE = EXT // 8
T_COARSE = T_FINE // 2
CROWS = ROWS // 2
T_CHAIN = (CROWS + 32) // 8
LOW, HIGH = 16, 112
OWN, FROM_N, FROM_S, FROM_L, FROM_R, SLOT, SHALLOW = 0, 12, 15, 18, 19, 21, 19
FROM_NL, FROM_NR, FROM_SL, FROM_SR = range(4)
R_N, R_S, R_L, R_R, R_NL, R_NR, R_SL, R_SR, R_ALL = 0, 18, 36, 48, 60, 61, 62, 63, 64


def roll(x, shift, axis):
    shift = shift % x.shape[axis]
    return pltpu.roll(x, shift, axis) if shift else x


def flux_pass(src, coef, drift, T, W, emit):
    def load(t):
        values = [src[t, w] for w in range(W)]
        return values, [coef[t, w] * (2.0 + jnp.tanh(values[w])) for w in range(W)]

    def flux(v, k, vn, kn):
        return (k + kn) * (vn - v)

    first, last = load(0), load(T - 1)
    final = [flux(last[0][w], last[1][w], roll(first[0][w], -1, 0), roll(first[1][w], -1, 0)) for w in range(W)]
    above = [roll(f, 1, 0) for f in final]
    here = first
    for t in range(T):
        v, k = here
        if t < T - 1:
            following = last if t + 1 == T - 1 else load(t + 1)
            below = [flux(v[w], k[w], following[0][w], following[1][w]) for w in range(W)]
        else:
            following, below = None, final
        east = [flux(v[w], k[w], v[w + 1], k[w + 1]) for w in range(W - 1)]
        east.append(flux(v[W - 1], k[W - 1], roll(v[0], -1, 1), roll(k[0], -1, 1)))
        west = [roll(east[W - 1], 1, 1)] + east[:-1]
        for w in range(W):
            emit(t, w, v[w], drift[t, w] + ((east[w] - west[w]) + (below[w] - above[w])))
        here, above = following, below


def heun(state, section, coef, drift, T, W, lanes, row_masks, emit=None):
    def keep(t, w, x):
        if w in (0, W - 1):
            x = x * lanes
        if t in row_masks:
            x = x * row_masks[t]
        return x

    def first(t, w, value, increment):
        middle = value + increment
        state[t, w] = middle
        section[t, w] = keep(t, w, middle + increment)

    def second(t, w, value, increment):
        result = keep(t, w, state[t, w] + increment)
        if emit is None:
            state[t, w] = result
        else:
            emit(t, w, result)

    flux_pass(state, coef, drift, T, W, first)
    flux_pass(section, coef, drift, T, W, second)


def pieces(x):
    top = x.astype(jnp.bfloat16)
    rest = x - top.astype(jnp.float32)
    middle = rest.astype(jnp.bfloat16)
    low = (rest - middle.astype(jnp.float32)).astype(jnp.bfloat16)
    return top, middle, low


def move_columns(x, choice):
    top, middle, low = [jnp.dot(part, choice, preferred_element_type=jnp.float32) for part in pieces(x)]
    return (top + middle) + low


def skew(x, step, sublane):
    moved = [roll(x, step * k, 1) for k in range(4)]
    i = sublane & 3
    return jnp.where(i < 2, jnp.where(i == 0, moved[0], moved[1]), jnp.where(i == 2, moved[2], moved[3]))


def pack_group(x, own):
    return [jnp.where(own, x[k], roll(x[3], 96 - 32 * k, 1)) for k in range(3)]


def unpack_group(y, lane):
    parts = [roll(y[k], 32 * k - 96, 1) for k in range(3)]
    return list(y) + [jnp.where(lane < LOW + 32, parts[0], jnp.where(lane < LOW + 64, parts[1], parts[2]))]


def kernel(
    initial, guesses, conduct, source, out,
    X, Y, HX, SR, SC, SK, R1, V, A, CH, SD, SPREAD, GATHER, PROLONG, RN, RS, RX, RR, BASE, RV, CA, CC, CSD, NAT, SB, SE, EB, EE, NB,
    V12, A12, C12, S12, CN, CB, OUT,
    load_sem, store_sem, send1, recv1, send_relaxed, recv_relaxed, send3, recv3, send_coef, send_share, recv_share, ready,
):
    nt, nx, ny = lax.axis_size("tm"), lax.axis_size("sx"), lax.axis_size("sy")
    me, row, col = lax.axis_index("tm"), lax.axis_index("sx"), lax.axis_index("sy")
    chip, core = me // 2, lax.rem(me, 2)
    chips, last = nt // 2, nt - 1
    north, south = lax.rem(row + nx - 1, nx), lax.rem(row + 1, nx)
    left, right = lax.rem(col + ny - 1, ny), lax.rem(col + 1, ny)
    spatial = [(north, col), (south, col), (row, left), (row, right),
               (north, left), (north, right), (south, left), (south, right)]

    barrier = pltpu.get_barrier_semaphore()
    for r, c in spatial:
        pl.semaphore_signal(barrier, inc=1, device_id=(me, r, c), device_id_type=MESH)
    for step in range(1, nt):
        pl.semaphore_signal(barrier, inc=1, device_id=(lax.rem(me + step, nt), row, col), device_id_type=MESH)

    def await_vectors(ref, sem):
        pltpu.make_async_copy(ref, ref, sem).wait()

    @pl.when(me == last)
    def _():
        pltpu.make_async_copy(initial, X.at[0], load_sem).start()

    @pl.when(me != last)
    def _():
        pltpu.make_async_copy(guesses.at[0], X.at[0], load_sem).start()

    pltpu.make_async_copy(conduct, X.at[1], load_sem).start()
    pltpu.make_async_copy(source, X.at[2], load_sem).start()

    lane = lax.broadcasted_iota(jnp.int32, (8, 128), 1)
    sublane = lax.broadcasted_iota(jnp.int32, (8, 128), 0)
    one, zero = jnp.ones((8, 128), jnp.float32), jnp.zeros((8, 128), jnp.float32)
    own_lanes = jnp.logical_and(lane >= LOW, lane < HIGH)
    at_top, at_bottom, at_left, at_right = row == 0, row == nx - 1, col == 0, col == ny - 1
    in_lanes = jnp.where(jnp.logical_or(jnp.logical_and(lane < LOW, at_left), jnp.logical_and(lane >= HIGH, at_right)), zero, one)

    def strip_mask(which, edge):
        return jnp.where(jnp.logical_and(sublane == which, edge), zero, one)

    def fill(ref, rows, columns):
        ref[...] = jnp.where(rows == columns, 1.0, 0.0).astype(jnp.bfloat16)

    o = lax.broadcasted_iota(jnp.int32, (1, 512), 1)
    fill(SPREAD, lax.broadcasted_iota(jnp.int32, (COLS, 1), 0) + 64, (o & 127) * 4 + (o >> 7))
    o = lax.broadcasted_iota(jnp.int32, (COLS, 1), 0)
    k, l = o >> 7, o & 127
    inside = jnp.logical_and(l >= LOW, l < HIGH)
    packed_from = jnp.where(inside, 4 * l + k, 4 * (((l + 16) & 127) + LOW + 32 * k) + 3)
    fill(GATHER, packed_from, lax.broadcasted_iota(jnp.int32, (1, COLS), 1) + 64)
    o = lax.broadcasted_iota(jnp.int32, (256, 1), 0)
    fill(PROLONG, (o & 127) * 2 + (o >> 7), (lax.broadcasted_iota(jnp.int32, (1, COLS), 1) + 64) >> 1)

    pltpu.make_async_copy(X, X, load_sem).wait()

    for field, factor in ((0, None), (1, 0.125 * TIME_STEP), (2, 0.5 * TIME_STEP)):
        spread = move_columns(X[field], SPREAD[...])
        for w in range(4):
            part = spread[:, 128 * w:128 * w + 128]
            Y[field, w, HALO:HALO + ROWS, :] = part if factor is None else part * factor

    def own_block(field, w, rb):
        return Y[field, w, HALO + 8 * rb:HALO + 8 * rb + 8, :]

    for field in range(3):
        for side in range(2):
            for b in range(2):
                packed = pack_group([own_block(field, w, b if side == 0 else 14 + b) for w in range(4)], own_lanes)
                for k in range(3):
                    SR[side, field * 6 + b * 3 + k] = packed[k]
    eighth = lane // 8
    for field in range(3):
        for side in range(2):
            for quarter in range(4):
                packed = None
                for q in range(16):
                    block = own_block(field, q % 4, 4 * quarter + q // 4)
                    block = roll(block, 8 * q + 100 - LOW if side == 0 else 8 * q - (HIGH - 4), 1)
                    slot_of = (q + 12) % 16 if side == 0 else q
                    packed = block if packed is None else jnp.where(eighth == slot_of, block, packed)
                SC[side, quarter, field] = packed
    odd_slot = (lane & 4) != 0
    for side in range(2):
        for end, quarter in ((0, 0), (1, 3)):
            fields = [SC[side, quarter, field] for field in range(3)]
            if side == 1:
                half = (lane < 64) if end == 0 else (lane >= 64)
                pair = jnp.where(odd_slot, roll(fields[1], 4, 1), fields[0])
            else:
                half = ((lane + 32) & 127) < 64 if end == 0 else ((lane + 32) & 127) >= 64
                pair = jnp.where(odd_slot, fields[0], roll(fields[1], -4, 1))
            SK[side, end] = jnp.where(half, pair, roll(fields[2], 64, 1))

    def pack_coarse(which):
        def block(rb, w):
            return NAT[which, w, 8 + 8 * rb:16 + 8 * rb, :]

        for g in range(4):
            packed = pack_group([block(2 * g + i // 2, i % 2) for i in range(4)], own_lanes)
            for k in range(3):
                SB[which, 3 * g + k] = packed[k]
        for w in range(2):
            SB[which, 14 + w] = block(0, w)
            SB[which, 16 + w] = block(7, w)
        for side in range(2):
            packed = None
            for q in range(16):
                moved = roll(block(q // 2, q % 2), 8 * q - LOW if side == 0 else 8 * q - (HIGH - 8), 1)
                packed = moved if packed is None else jnp.where(eighth == q, moved, packed)
            SB[which, 12 + side] = packed
            for end in range(2):
                moved = skew(roll(packed, 32 if end else 0, 1), 32, sublane)
                moved = jnp.where((lane // 32) == (sublane & 3), moved, 0.0)
                moved = moved + roll(moved, 1, 0)
                moved = moved + roll(moved, 2, 0)
                SE[which, 2 * side + end, 0:1, :] = moved[3:4, :]
                SE[which, 2 * side + end, 1:2, :] = moved[7:8, :]

    def coarse_copies(which, slot, tm, send, recv, deep=True):
        def copy(src, dst, where):
            return pltpu.make_async_remote_copy(src, dst, send, recv, (tm,) + where, MESH)

        def vectors(a, size, k, where):
            return copy(SB.at[which, a:a + size], EB.at[slot, k:k + size], where)

        return [
            copy(SE.at[which, 0], EE.at[slot, FROM_SR], (north, left)),
            copy(SE.at[which, 2], EE.at[slot, FROM_SL], (north, right)),
            copy(SE.at[which, 1], EE.at[slot, FROM_NR], (south, left)),
            copy(SE.at[which, 3], EE.at[slot, FROM_NL], (south, right)),
            vectors(0, 3, FROM_S, (north, col)) if deep else vectors(14, 2, FROM_S, (north, col)),
            vectors(9, 3, FROM_N, (south, col)) if deep else vectors(16, 2, FROM_N, (south, col)),
            vectors(12, 1, FROM_R, (row, left)),
            vectors(13, 1, FROM_L, (row, right)),
            vectors(0, 12, OWN, (row, col)),
        ]

    coef_copies = [copy for k in (1, 2) for copy in coarse_copies(k, 6 + k, me, send_coef, recv3.at[7])[:8]]

    @pl.when(core == 1)
    def _():
        for k in (1, 2):
            for rb in range(8):
                for w in range(2):
                    def at(ww, r):
                        return Y[k, ww, pl.ds(HALO + 16 * rb + r, 8, stride=2), :]
                    total = (at(2 * w, 0) + at(2 * w + 1, 0)) + (at(2 * w, 1) + at(2 * w + 1, 1))
                    NAT[k, w, 8 + 8 * rb:16 + 8 * rb, :] = 0.25 * total if k == 1 else total
            pack_coarse(k)
            for v in range(12):
                EB[6 + k, v] = SB[k, v]

    pl.semaphore_wait(barrier, 8 + nt - 1)

    first_exchange = [
        pltpu.make_async_remote_copy(s, R1.at[k:k + size], send1, recv1, (me,) + w, MESH)
        for s, k, size, w in [
            (SK.at[1, 1:2], R_NL, 1, (south, right)),
            (SK.at[0, 1:2], R_NR, 1, (south, left)),
            (SK.at[1, 0:1], R_SL, 1, (north, right)),
            (SK.at[0, 0:1], R_SR, 1, (north, left)),
            (SR.at[0], R_S, 18, (north, col)),
            (SR.at[1], R_N, 18, (south, col)),
        ]
    ]
    for side, k, w in ((1, R_L, (row, right)), (0, R_R, (row, left))):
        for quarter in range(4):
            first_exchange.append(pltpu.make_async_remote_copy(
                SC.at[side, quarter], R1.at[k + 3 * quarter:k + 3 * quarter + 3], send1, recv1, (me,) + w, MESH))
    for copy in first_exchange:
        copy.start()

    @pl.when(core == 1)
    def _():
        for copy in coef_copies:
            copy.start()

    pltpu.make_async_copy(R1, R1, recv1).wait()

    for step in range(1, nt):
        pl.semaphore_signal(ready, inc=1, device_id=(lax.rem(me + step, nt), row, col), device_id_type=MESH)

    top16, bottom16 = strip_mask(0, at_top), strip_mask(7, at_bottom)
    masks = [in_lanes * (top16 if t < HALO else 1.0) * (bottom16 if t >= T_FINE - HALO else 1.0) for t in range(T_FINE)]
    for field, dest in ((1, CH), (0, V), (2, SD)):
        halo = {}
        for e in range(EXT // 8):
            if e < 2:
                l, r, rb = R_NL, R_NR, 14 + e
            elif e >= 18:
                l, r, rb = R_SL, R_SR, e - 18
            else:
                rb = e - 2
                l, r = R_L + 3 * (rb // 4), R_R + 3 * (rb // 4)
            if (l, r) not in halo:
                if e < 2 or e >= 18:
                    shift = (0, 4, 64)[field]
                    halo[l, r] = jnp.where(odd_slot, roll(R1[r], shift, 1), roll(R1[l], -shift, 1))
                else:
                    halo[l, r] = jnp.where(odd_slot, R1[r + field], R1[l + field])
            if e < 2 or e >= 18:
                start = (R_N + e * 3 if e < 2 else R_S + (e - 18) * 3) + field * 6
                values = unpack_group([R1[start + k] for k in range(3)], lane)
                for w in range(4):
                    Y[field, w, 8 * e:8 * e + 8, :] = values[w]
            HX[field, 8 * e:8 * e + 8, :] = roll(halo[l, r], -32 * (rb % 4), 1)
        for t in range(T_FINE):
            around = HX[field, pl.ds(t, 8, stride=T_FINE), :]
            for w in range(4):
                value = Y[field, w, pl.ds(t, 8, stride=T_FINE), :]
                dest[t, w] = jnp.where(own_lanes, value, roll(around, LOW - 4 - 8 * w, 1)) * masks[t]

    def four(ref, t, w):
        return (ref[2 * t, 2 * w] + ref[2 * t, 2 * w + 1]) + (ref[2 * t + 1, 2 * w] + ref[2 * t + 1, 2 * w + 1])

    for t in range(T_COARSE):
        for w in range(2):
            CC[t, w] = 0.25 * four(CH, t, w)
            CSD[t, w] = four(SD, t, w)

    fine_rows = {HALO - 1: top16, T_FINE - HALO: bottom16}

    def fine_run():
        def body(i, carry):
            heun(V, A, CH, SD, T_FINE, 4, in_lanes, fine_rows)
            return carry

        lax.fori_loop(0, FINE, body, 0)

    fine_run()

    for t in range(T_FINE):
        for w in range(4):
            RN[w, pl.ds(t, 8, stride=T_FINE), :] = V[t, w]
    for rb in range(16):
        packed = pack_group([RN[w, HALO + 8 * rb:HALO + 8 * rb + 8, :] for w in range(4)], own_lanes)
        for k in range(3):
            RS[k, 8 * rb:8 * rb + 8, :] = packed[k]
    relaxed_copy = pltpu.make_async_remote_copy(
        RS, RX, send_relaxed, recv_relaxed, (lax.rem(me + 1, nt), row, col), MESH)
    relaxed_copy.start()
    for t in range(T_COARSE):
        for w in range(2):
            RV[t, w] = 0.25 * four(V, t, w)

    fine_run()

    share_of_psi = jnp.where(me == last, 0.0, 1.0)

    def target(t, w, result):
        NAT[0, w, pl.ds(t, 8, stride=T_COARSE), :] = 0.25 * four(V, t, w) - share_of_psi * result

    coarse_rows = {HALO // 2 - 1: top16, T_COARSE - HALO // 2: bottom16}
    heun(RV, CA, CC, CSD, T_COARSE, 2, in_lanes, coarse_rows, target)
    pack_coarse(0)
    pl.semaphore_wait(ready, nt - 1)

    slot_out = jnp.where(me == last, 0, me + 1)
    is_last = me == last

    def each_receiver(action):
        for k in (0, 3, 2, 1):
            shallow, deep = [
                coarse_copies(0, slot_out, 2 * lax.rem(chip + k, chips) + 1, send3.at[k], recv3.at[slot_out], deep)
                for deep in (False, True)]
            if k == 0:
                @pl.when(is_last)
                def _():
                    action(k, deep[:8], SLOT - FROM_N)
                continue
            reached = jnp.logical_or(is_last, jnp.logical_and(chip + k < chips, me < last - 1))
            special = me == 0 if k == 3 else core == 1 if k == 1 else None

            @pl.when(reached if special is None else jnp.logical_and(reached, jnp.logical_not(special)))
            def _():
                action(k, shallow, SHALLOW)

            if special is not None:
                @pl.when(jnp.logical_and(reached, special))
                def _():
                    if k == 3:
                        action(k, deep, SLOT)
                    else:
                        action(k, shallow[8:], FROM_N)

    def start(k, copies, vectors):
        for copy in copies:
            copy.start()

    def finish(k, copies, vectors):
        await_vectors(EB.at[0, 0:vectors], send3.at[k])

    each_receiver(start)

    def unpack(slot, store, deep=True):
        def halo_at(e):
            if e < 2:
                return corners[FROM_NL], corners[FROM_NR], e
            if e >= 10:
                return corners[FROM_SL], corners[FROM_SR], e - 10
            return EB[slot, FROM_L], EB[slot, FROM_R], e - 2

        corners = []
        for k in range(4):
            two = jnp.where(sublane < 4, EE[slot, k, 0:1, :], EE[slot, k, 1:2, :])
            corners.append(skew(two, -32, sublane))

        for g in range(6):
            base = FROM_N if g == 0 else FROM_S if g == 5 else OWN + 3 * (g - 1)
            three = [EB[slot, base + k] for k in range(3)]
            values = unpack_group(three, lane)
            if g in (0, 5):
                values = [jnp.where(deep, values[i], three[i % 2]) for i in range(4)]
            mask = in_lanes
            if g == 0:
                mask = mask * jnp.where(at_top, 0.0, 1.0)
            if g == 5:
                mask = mask * jnp.where(at_bottom, 0.0, 1.0)
            for i in range(4):
                e, w = 2 * g + i // 2, i % 2
                from_left, from_right, rb = halo_at(e)
                q = rb * 2 + w
                value = jnp.where(lane < LOW, roll(from_left, LOW - 8 - 8 * q, 1), values[i])
                value = jnp.where(lane >= HIGH, roll(from_right, HIGH - 8 * q, 1), value)
                NB[w, 8 * e:8 * e + 8, :] = value * mask
        for t in range(T_CHAIN):
            for w in range(2):
                store(t, w, NB[w, pl.ds(t, 8, stride=T_CHAIN), :])

    chain_rows = {15 % T_CHAIN: strip_mask(15 // T_CHAIN, at_top), 80 % T_CHAIN: strip_mask(80 // T_CHAIN, at_bottom)}
    share = pltpu.make_async_remote_copy(
        CB, CN, send_share, recv_share, (jnp.maximum(me - 1, 0), row, col), MESH)

    def natural(ref):
        for t in range(T_CHAIN):
            for w in range(2):
                NB[w, pl.ds(t, 8, stride=T_CHAIN), :] = V12[t, w]
        for w in range(2):
            ref[w] = NB[w, 16:16 + CROWS, :]

    def relaxed_base():
        await_vectors(RX, recv_relaxed)
        for rb in range(16):
            values = unpack_group([RX[k, 8 * rb:8 * rb + 8, :] for k in range(3)], lane)
            for w in range(4):
                RN[w, 8 * rb:8 * rb + 8, :] = values[w]
        for t in range(8):
            for w in range(2):
                def at(tt, ww):
                    return RN[ww, pl.ds(tt, 8, stride=16), :]
                RR[t, w] = 0.25 * ((at(2 * t, 2 * w) + at(2 * t, 2 * w + 1)) + (at(2 * t + 1, 2 * w) + at(2 * t + 1, 2 * w + 1)))
        base = move_columns(jnp.concatenate([RX[k] for k in range(3)], axis=1), GATHER[...])
        for k in range(3):
            BASE[k] = base[:, 128 * k:128 * k + 128]

    @pl.when(core == 1)
    def _():
        def put(ref):
            def store(t, w, x):
                ref[t, w] = x
            return store

        await_vectors(EB.at[7:9, FROM_N:SLOT], recv3.at[7])
        unpack(7, put(C12))
        unpack(8, put(S12))

    relaxed_base()

    @pl.when(core == 1)
    def _():
        def put(t, w, x):
            V12[t, w] = x

        def add(t, w, x):
            V12[t, w] = V12[t, w] + x

        @pl.when(is_last)
        def _():
            for v in range(12):
                EB[0, v] = SB[0, v]
            await_vectors(EB.at[0, FROM_N:SLOT], recv3.at[0])

        @pl.when(me == 1)
        def _():
            await_vectors(EB.at[0, 0:FROM_N], recv3.at[0])

        @pl.when(jnp.logical_and(me != last, me > 1))
        def _():
            await_vectors(EB.at[0, 0:SHALLOW], recv3.at[0])

        unpack(0, put, is_last)

        @pl.when(me > 1)
        def _():
            heun(V12, A12, C12, S12, T_CHAIN, 2, in_lanes, chain_rows)

            @pl.when(is_last)
            def _():
                await_vectors(EB.at[1], recv3.at[1])

            @pl.when(jnp.logical_not(is_last))
            def _():
                await_vectors(EB.at[1, 0:SHALLOW], recv3.at[1])

            unpack(1, add, is_last)

        def body(slot, carry):
            final = slot == me - 1

            @pl.when(final)
            def _():
                natural(CB)
                share.start()
                await_vectors(EB.at[slot, 0:FROM_N], recv3.at[slot])

            @pl.when(jnp.logical_not(final))
            def _():
                await_vectors(EB.at[slot, 0:SHALLOW], recv3.at[slot])

            heun(V12, A12, C12, S12, T_CHAIN, 2, in_lanes, chain_rows)
            unpack(slot, add, False)
            return carry

        lax.fori_loop(2, me, body, 0)
        natural(CN)

        @pl.when(me > 1)
        def _():
            share.wait_send()

    @pl.when(jnp.logical_and(core == 0, me > 0))
    def _():
        share.wait_recv()

    @pl.when(me == 0)
    def _():
        for t in range(8):
            for w in range(2):
                CN[w, pl.ds(t, 8, stride=8), :] = RR[t, w]

    change = jnp.concatenate(
        [jnp.concatenate([jnp.where(own_lanes, CN[w, pl.ds(t, 8, stride=8), :] - RR[t, w], 0.0) for w in range(2)], axis=1)
         for t in range(8)], axis=0)
    change = move_columns(change, PROLONG[...])
    for t in range(8):
        for k in range(3):
            for tt in (2 * t, 2 * t + 1):
                OUT[k, pl.ds(tt, 8, stride=16), :] = (
                    BASE[k, pl.ds(tt, 8, stride=16), :] + change[8 * t:8 * t + 8, 128 * k:128 * k + 128])
    for k in range(3):
        pltpu.make_async_copy(OUT.at[k], out.at[0, :, 128 * k:128 * k + 128], store_sem).start()

    await_vectors(R1, send1)

    @pl.when(core == 1)
    def _():
        await_vectors(EB.at[7:9, FROM_N:SLOT], send_coef)

    relaxed_copy.wait_send()
    each_receiver(finish)
    await_vectors(OUT, store_sem)


def local(initial, guesses, conduct, source):
    nt = lax.axis_size("tm")
    f32, bf16 = jnp.float32, jnp.bfloat16
    vmem, dma = pltpu.VMEM, pltpu.SemaphoreType.DMA
    fine, coarse, chain = (T_FINE, 4, 8, 128), (T_COARSE, 2, 8, 128), (T_CHAIN, 2, 8, 128)
    scratch = [
        vmem((3, ROWS, COLS), f32),
        vmem((3, 4, EXT, 128), f32),
        vmem((3, EXT, 128), f32),
        vmem((2, 18, 8, 128), f32),
        vmem((2, 4, 3, 8, 128), f32),
        vmem((2, 2, 8, 128), f32),
        vmem((R_ALL, 8, 128), f32),
        vmem(fine, f32),
        vmem(fine, f32),
        vmem(fine, f32),
        vmem(fine, f32),
        vmem((COLS, 512), bf16),
        vmem((COLS, COLS), bf16),
        vmem((256, COLS), bf16),
        vmem((4, EXT, 128), f32),
        vmem((3, ROWS, 128), f32),
        vmem((3, ROWS, 128), f32),
        vmem((8, 2, 8, 128), f32),
        vmem((3, ROWS, 128), f32),
        vmem(coarse, f32),
        vmem(coarse, f32),
        vmem(coarse, f32),
        vmem(coarse, f32),
        vmem((3, 2, EXT // 2, 128), f32),
        vmem((3, 18, 8, 128), f32),
        vmem((3, 4, 2, 128), f32),
        vmem((9, SLOT, 8, 128), f32),
        vmem((9, 4, 2, 128), f32),
        vmem((2, CROWS + 32, 128), f32),
        vmem(chain, f32),
        vmem(chain, f32),
        vmem(chain, f32),
        vmem(chain, f32),
        vmem((2, CROWS, 128), f32),
        vmem((2, CROWS, 128), f32),
        vmem((3, ROWS, 128), f32),
        dma, dma, dma, dma, dma, dma, dma((nt // 2,)), dma((8,)), dma, dma, dma,
        pltpu.SemaphoreType.REGULAR,
    ]
    return pl.pallas_call(
        kernel,
        out_shape=jax.ShapeDtypeStruct(guesses.shape, f32),
        in_specs=[pl.BlockSpec(memory_space=pl.ANY)] * 4,
        out_specs=pl.BlockSpec(memory_space=pl.ANY),
        scratch_shapes=scratch,
        compiler_params=pltpu.CompilerParams(collective_id=0, has_side_effects=True, vmem_limit_bytes=54976 * 1024),
    )(initial, guesses, conduct, source)


def solution(mesh):
    in_specs = (P("sx", "sy"), P("tm", "sx", "sy"), P("sx", "sy"), P("sx", "sy"))
    out_specs = P("tm", "sx", "sy")
    return jax.shard_map(local, mesh=mesh, in_specs=in_specs, out_specs=out_specs, check_vma=False)
```

```python
import jax
import jax.numpy as jnp
from jax import lax
from jax.experimental import pallas as pl
from jax.experimental.pallas import tpu as pltpu
from jax.sharding import PartitionSpec as P

MESH = pl.DeviceIdType.MESH
FINE = 4
TIME_STEP = 0.035

ROWS, COLS, HALO = 128, 384, 16
EXT = ROWS + 2 * HALO
T_FINE = EXT // 8
T_COARSE = T_FINE // 2
CROWS = ROWS // 2
T_CHAIN = (CROWS + 32) // 8
LOW, HIGH = 16, 112
OWN, FROM_N, FROM_S, FROM_L, FROM_R, SLOT, SHALLOW = 0, 12, 15, 18, 19, 21, 19
FROM_NL, FROM_NR, FROM_SL, FROM_SR = range(4)
R_N, R_S, R_NL, R_NR, R_SL, R_SR, R_L, R_R, R_ALL = 0, 18, 36, 37, 38, 39, 40, 52, 64


def roll(x, shift, axis):
    shift = shift % x.shape[axis]
    return pltpu.roll(x, shift, axis) if shift else x


def flux_pass(src, coef, drift, T, W, emit):
    def load(t):
        values = [src[t, w] for w in range(W)]
        return values, [coef[t, w] * (2.0 + jnp.tanh(values[w])) for w in range(W)]

    def flux(v, k, vn, kn):
        return (k + kn) * (vn - v)

    first, last = load(0), load(T - 1)
    final = [flux(last[0][w], last[1][w], roll(first[0][w], -1, 0), roll(first[1][w], -1, 0)) for w in range(W)]
    above = [roll(f, 1, 0) for f in final]
    here = first
    for t in range(T):
        v, k = here
        if t < T - 1:
            following = last if t + 1 == T - 1 else load(t + 1)
            below = [flux(v[w], k[w], following[0][w], following[1][w]) for w in range(W)]
        else:
            following, below = None, final
        east = [flux(v[w], k[w], v[w + 1], k[w + 1]) for w in range(W - 1)]
        east.append(flux(v[W - 1], k[W - 1], roll(v[0], -1, 1), roll(k[0], -1, 1)))
        west = [roll(east[W - 1], 1, 1)] + east[:-1]
        for w in range(W):
            emit(t, w, v[w], drift[t, w] + ((east[w] - west[w]) + (below[w] - above[w])))
        here, above = following, below


def heun(state, section, coef, drift, T, W, lanes, row_masks, emit=None):
    def keep(t, w, x):
        if w in (0, W - 1):
            x = x * lanes
        if t in row_masks:
            x = x * row_masks[t]
        return x

    def first(t, w, value, increment):
        middle = value + increment
        state[t, w] = middle
        section[t, w] = keep(t, w, middle + increment)

    def second(t, w, value, increment):
        result = keep(t, w, state[t, w] + increment)
        if emit is None:
            state[t, w] = result
        else:
            emit(t, w, result)

    flux_pass(state, coef, drift, T, W, first)
    flux_pass(section, coef, drift, T, W, second)


def pieces(x):
    top = x.astype(jnp.bfloat16)
    rest = x - top.astype(jnp.float32)
    middle = rest.astype(jnp.bfloat16)
    low = (rest - middle.astype(jnp.float32)).astype(jnp.bfloat16)
    return top, middle, low


def move_columns(x, choice):
    moved = jnp.dot(jnp.concatenate(pieces(x), axis=0), choice, preferred_element_type=jnp.float32)
    n = x.shape[0]
    return (moved[:n] + moved[n:2 * n]) + moved[2 * n:]


def skew(x, step, sublane):
    moved = [roll(x, step * k, 1) for k in range(4)]
    i = sublane & 3
    return jnp.where(i < 2, jnp.where(i == 0, moved[0], moved[1]), jnp.where(i == 2, moved[2], moved[3]))


def pack_group(x, own):
    return [jnp.where(own, x[k], roll(x[3], 96 - 32 * k, 1)) for k in range(3)]


def unpack_group(y, lane):
    parts = [roll(y[k], 32 * k - 96, 1) for k in range(3)]
    return list(y) + [jnp.where(lane < LOW + 32, parts[0], jnp.where(lane < LOW + 64, parts[1], parts[2]))]


def kernel(
    initial, guesses, conduct, source, out,
    X, Y, HX, SR, SC, SK, R1, V, A, CH, SD, SPREAD, GATHER, PROLONG, RN, RS, RX, RR, BASE, RV, CA, CC, CSD, NAT, SB, SE, EB, EE, NB,
    V12, A12, C12, S12, CN, CB, OUT,
    load_sem, send1, recv1, send_relaxed, recv_relaxed, send3, recv3, send_coef, send_share, recv_share, ready,
):
    nt, nx, ny = lax.axis_size("tm"), lax.axis_size("sx"), lax.axis_size("sy")
    me, row, col = lax.axis_index("tm"), lax.axis_index("sx"), lax.axis_index("sy")
    chip, core = me // 2, lax.rem(me, 2)
    chips, last = nt // 2, nt - 1
    north, south = lax.rem(row + nx - 1, nx), lax.rem(row + 1, nx)
    left, right = lax.rem(col + ny - 1, ny), lax.rem(col + 1, ny)
    spatial = [(north, col), (south, col), (row, left), (row, right),
               (north, left), (north, right), (south, left), (south, right)]

    barrier = pltpu.get_barrier_semaphore()
    for r, c in reversed(spatial):
        pl.semaphore_signal(barrier, inc=1, device_id=(me, r, c), device_id_type=MESH)
    for step in range(1, nt):
        pl.semaphore_signal(barrier, inc=1, device_id=(lax.rem(me + step, nt), row, col), device_id_type=MESH)

    def await_vectors(ref, sem):
        pltpu.make_async_copy(ref, ref, sem).wait()

    @pl.when(me == last)
    def _():
        pltpu.make_async_copy(initial, X.at[0], load_sem).start()

    @pl.when(me != last)
    def _():
        pltpu.make_async_copy(guesses.at[0], X.at[0], load_sem).start()

    pltpu.make_async_copy(conduct, X.at[1], load_sem).start()
    pltpu.make_async_copy(source, X.at[2], load_sem).start()

    lane = lax.broadcasted_iota(jnp.int32, (8, 128), 1)
    sublane = lax.broadcasted_iota(jnp.int32, (8, 128), 0)
    one, zero = jnp.ones((8, 128), jnp.float32), jnp.zeros((8, 128), jnp.float32)
    own_lanes = jnp.logical_and(lane >= LOW, lane < HIGH)
    at_top, at_bottom, at_left, at_right = row == 0, row == nx - 1, col == 0, col == ny - 1
    in_lanes = jnp.where(jnp.logical_or(jnp.logical_and(lane < LOW, at_left), jnp.logical_and(lane >= HIGH, at_right)), zero, one)

    def strip_mask(which, edge):
        return jnp.where(jnp.logical_and(sublane == which, edge), zero, one)

    def fill(ref, rows, columns):
        ref[...] = jnp.where(rows == columns, 1.0, 0.0).astype(jnp.bfloat16)

    o = lax.broadcasted_iota(jnp.int32, (1, 512), 1)
    fill(SPREAD, lax.broadcasted_iota(jnp.int32, (COLS, 1), 0) + 64, (o & 127) * 4 + (o >> 7))
    o = lax.broadcasted_iota(jnp.int32, (COLS, 1), 0)
    k, l = o >> 7, o & 127
    inside = jnp.logical_and(l >= LOW, l < HIGH)
    packed_from = jnp.where(inside, 4 * l + k, 4 * (((l + 16) & 127) + LOW + 32 * k) + 3)
    fill(GATHER, packed_from, lax.broadcasted_iota(jnp.int32, (1, COLS), 1) + 64)
    o = lax.broadcasted_iota(jnp.int32, (256, 1), 0)
    fill(PROLONG, (o & 127) * 2 + (o >> 7), (lax.broadcasted_iota(jnp.int32, (1, COLS), 1) + 64) >> 1)

    pltpu.make_async_copy(X, X, load_sem).wait()

    for field, factor in ((0, None), (1, 0.125 * TIME_STEP), (2, 0.5 * TIME_STEP)):
        spread = move_columns(X[field], SPREAD[...])
        for w in range(4):
            part = spread[:, 128 * w:128 * w + 128]
            Y[field, w, HALO:HALO + ROWS, :] = part if factor is None else part * factor

    def own_block(field, w, rb):
        return Y[field, w, HALO + 8 * rb:HALO + 8 * rb + 8, :]

    for field in range(3):
        for side in range(2):
            for b in range(2):
                packed = pack_group([own_block(field, w, b if side == 0 else 14 + b) for w in range(4)], own_lanes)
                for k in range(3):
                    SR[side, field * 6 + b * 3 + k] = packed[k]
    eighth = lane // 8
    for field in range(3):
        for side in range(2):
            for quarter in range(4):
                packed = None
                for q in range(16):
                    block = own_block(field, q % 4, 4 * quarter + q // 4)
                    block = roll(block, 8 * q + 100 - LOW if side == 0 else 8 * q - (HIGH - 4), 1)
                    slot_of = (q + 12) % 16 if side == 0 else q
                    packed = block if packed is None else jnp.where(eighth == slot_of, block, packed)
                SC[side, quarter, field] = packed
    odd_slot = (lane & 4) != 0
    for side in range(2):
        for end, quarter in ((0, 0), (1, 3)):
            fields = [SC[side, quarter, field] for field in range(3)]
            if side == 1:
                half = (lane < 64) if end == 0 else (lane >= 64)
                pair = jnp.where(odd_slot, roll(fields[1], 4, 1), fields[0])
            else:
                half = ((lane + 32) & 127) < 64 if end == 0 else ((lane + 32) & 127) >= 64
                pair = jnp.where(odd_slot, fields[0], roll(fields[1], -4, 1))
            SK[side, end] = jnp.where(half, pair, roll(fields[2], 64, 1))

    def pack_coarse(which):
        def block(rb, w):
            return NAT[which, w, 8 + 8 * rb:16 + 8 * rb, :]

        for g in range(4):
            packed = pack_group([block(2 * g + i // 2, i % 2) for i in range(4)], own_lanes)
            for k in range(3):
                SB[which, 3 * g + k] = packed[k]
        for w in range(2):
            SB[which, 14 + w] = block(0, w)
            SB[which, 16 + w] = block(7, w)
        for side in range(2):
            packed = None
            for q in range(16):
                moved = roll(block(q // 2, q % 2), 8 * q - LOW if side == 0 else 8 * q - (HIGH - 8), 1)
                packed = moved if packed is None else jnp.where(eighth == q, moved, packed)
            SB[which, 12 + side] = packed
            for end in range(2):
                moved = skew(roll(packed, 32 if end else 0, 1), 32, sublane)
                moved = jnp.where((lane // 32) == (sublane & 3), moved, 0.0)
                moved = moved + roll(moved, 1, 0)
                moved = moved + roll(moved, 2, 0)
                SE[which, 2 * side + end, 0:1, :] = moved[3:4, :]
                SE[which, 2 * side + end, 1:2, :] = moved[7:8, :]

    def coarse_copies(which, slot, tm, send, recv, deep=True):
        def copy(src, dst, where):
            return pltpu.make_async_remote_copy(src, dst, send, recv, (tm,) + where, MESH)

        def vectors(a, size, k, where):
            return copy(SB.at[which, a:a + size], EB.at[slot, k:k + size], where)

        return [
            copy(SE.at[which, 0], EE.at[slot, FROM_SR], (north, left)),
            copy(SE.at[which, 2], EE.at[slot, FROM_SL], (north, right)),
            copy(SE.at[which, 1], EE.at[slot, FROM_NR], (south, left)),
            copy(SE.at[which, 3], EE.at[slot, FROM_NL], (south, right)),
            vectors(0, 3, FROM_S, (north, col)) if deep else vectors(14, 2, FROM_S, (north, col)),
            vectors(9, 3, FROM_N, (south, col)) if deep else vectors(16, 2, FROM_N, (south, col)),
            vectors(12, 1, FROM_R, (row, left)),
            vectors(13, 1, FROM_L, (row, right)),
            vectors(0, 12, OWN, (row, col)),
        ]

    pl.semaphore_wait(barrier, 8 + nt - 1)

    first_exchange = [
        pltpu.make_async_remote_copy(s, R1.at[k:k + size], send1, recv1.at[0], (me,) + w, MESH)
        for s, k, size, w in [
            (SK.at[1, 1:2], R_NL, 1, (south, right)),
            (SK.at[0, 1:2], R_NR, 1, (south, left)),
            (SK.at[1, 0:1], R_SL, 1, (north, right)),
            (SK.at[0, 0:1], R_SR, 1, (north, left)),
            (SR.at[0], R_S, 18, (north, col)),
            (SR.at[1], R_N, 18, (south, col)),
        ]
    ]
    for side, k, w in ((1, R_L, (row, right)), (0, R_R, (row, left))):
        for quarter in range(4):
            first_exchange.append(pltpu.make_async_remote_copy(
                SC.at[side, quarter], R1.at[k + 3 * quarter:k + 3 * quarter + 3], send1, recv1.at[1], (me,) + w, MESH))
    for copy in first_exchange:
        copy.start()

    coef_copies = [copy for k in (1, 2) for copy in coarse_copies(k, 6 + k, me, send_coef, recv3.at[7])[:8]]

    @pl.when(core == 1)
    def _():
        for k in (1, 2):
            for rb in range(8):
                for w in range(2):
                    def at(ww, r):
                        return Y[k, ww, pl.ds(HALO + 16 * rb + r, 8, stride=2), :]
                    total = (at(2 * w, 0) + at(2 * w + 1, 0)) + (at(2 * w, 1) + at(2 * w + 1, 1))
                    NAT[k, w, 8 + 8 * rb:16 + 8 * rb, :] = 0.25 * total if k == 1 else total
            pack_coarse(k)
            for v in range(12):
                EB[6 + k, v] = SB[k, v]
        for copy in coef_copies:
            copy.start()

    await_vectors(R1.at[R_L:R_ALL], recv1.at[1])
    for field in range(3):
        for rb in range(16):
            l, r = R_L + 3 * (rb // 4) + field, R_R + 3 * (rb // 4) + field
            around = jnp.where(odd_slot, R1[r], R1[l])
            HX[field, 8 * rb + HALO:8 * rb + HALO + 8, :] = roll(around, -32 * (rb % 4), 1)
    await_vectors(R1.at[0:R_L], recv1.at[0])

    for step in range(1, nt):
        pl.semaphore_signal(ready, inc=1, device_id=(lax.rem(me + step, nt), row, col), device_id_type=MESH)

    top16, bottom16 = strip_mask(0, at_top), strip_mask(7, at_bottom)
    masks = [in_lanes * (top16 if t < HALO else 1.0) * (bottom16 if t >= T_FINE - HALO else 1.0) for t in range(T_FINE)]
    for field, dest in ((1, CH), (0, V), (2, SD)):
        for e in (0, 1, 18, 19):
            l, r, rb = (R_NL, R_NR, 14 + e) if e < 2 else (R_SL, R_SR, e - 18)
            shift = (0, 4, 64)[field]
            corners = jnp.where(odd_slot, roll(R1[r], shift, 1), roll(R1[l], -shift, 1))
            start = (R_N + e * 3 if e < 2 else R_S + (e - 18) * 3) + field * 6
            values = unpack_group([R1[start + k] for k in range(3)], lane)
            for w in range(4):
                Y[field, w, 8 * e:8 * e + 8, :] = values[w]
            HX[field, 8 * e:8 * e + 8, :] = roll(corners, -32 * (rb % 4), 1)
        for t in range(T_FINE):
            around = HX[field, pl.ds(t, 8, stride=T_FINE), :]
            for w in range(4):
                value = Y[field, w, pl.ds(t, 8, stride=T_FINE), :]
                dest[t, w] = jnp.where(own_lanes, value, roll(around, LOW - 4 - 8 * w, 1)) * masks[t]

    def four(ref, t, w):
        return (ref[2 * t, 2 * w] + ref[2 * t, 2 * w + 1]) + (ref[2 * t + 1, 2 * w] + ref[2 * t + 1, 2 * w + 1])

    for t in range(T_COARSE):
        for w in range(2):
            CC[t, w] = 0.25 * four(CH, t, w)
            CSD[t, w] = four(SD, t, w)

    fine_rows = {HALO - 1: top16, T_FINE - HALO: bottom16}

    def fine_run():
        def body(i, carry):
            heun(V, A, CH, SD, T_FINE, 4, in_lanes, fine_rows)
            return carry

        lax.fori_loop(0, FINE, body, 0)

    fine_run()

    for t in range(T_FINE):
        for w in range(4):
            RN[w, pl.ds(t, 8, stride=T_FINE), :] = V[t, w]
    for rb in range(16):
        packed = pack_group([RN[w, HALO + 8 * rb:HALO + 8 * rb + 8, :] for w in range(4)], own_lanes)
        for k in range(3):
            RS[k, 8 * rb:8 * rb + 8, :] = packed[k]
    relaxed_copy = pltpu.make_async_remote_copy(
        RS, RX, send_relaxed, recv_relaxed, (lax.rem(me + 1, nt), row, col), MESH)
    relaxed_copy.start()
    for t in range(T_COARSE):
        for w in range(2):
            RV[t, w] = 0.25 * four(V, t, w)

    fine_run()

    share_of_psi = jnp.where(me == last, 0.0, 1.0)

    def target(t, w, result):
        NAT[0, w, pl.ds(t, 8, stride=T_COARSE), :] = 0.25 * four(V, t, w) - share_of_psi * result

    coarse_rows = {HALO // 2 - 1: top16, T_COARSE - HALO // 2: bottom16}
    heun(RV, CA, CC, CSD, T_COARSE, 2, in_lanes, coarse_rows, target)
    pack_coarse(0)
    pl.semaphore_wait(ready, nt - 1)

    slot_out = jnp.where(me == last, 0, me + 1)
    is_last = me == last

    def each_receiver(action):
        for k in (3, 2, 0, 1):
            shallow, deep = [
                coarse_copies(0, slot_out, 2 * lax.rem(chip + k, chips) + 1, send3.at[k], recv3.at[slot_out], deep)
                for deep in (False, True)]
            if k == 0:
                @pl.when(is_last)
                def _():
                    action(k, deep[:8], SLOT - FROM_N)
                continue
            reached = jnp.logical_or(is_last, jnp.logical_and(chip + k < chips, me < last - 1))
            special = me == 0 if k == 3 else core == 1 if k == 1 else None

            @pl.when(reached if special is None else jnp.logical_and(reached, jnp.logical_not(special)))
            def _():
                action(k, shallow, SHALLOW)

            if special is not None:
                @pl.when(jnp.logical_and(reached, special))
                def _():
                    if k == 3:
                        action(k, deep, SLOT)
                    else:
                        action(k, shallow[8:], FROM_N)

    def start(k, copies, vectors):
        for copy in copies:
            copy.start()

    def finish(k, copies, vectors):
        await_vectors(EB.at[0, 0:vectors], send3.at[k])

    each_receiver(start)

    def unpack(slot, store, deep=True):
        def halo_at(e):
            if e < 2:
                return corners[FROM_NL], corners[FROM_NR], e
            if e >= 10:
                return corners[FROM_SL], corners[FROM_SR], e - 10
            return EB[slot, FROM_L], EB[slot, FROM_R], e - 2

        corners = []
        for k in range(4):
            two = jnp.where(sublane < 4, EE[slot, k, 0:1, :], EE[slot, k, 1:2, :])
            corners.append(skew(two, -32, sublane))

        for g in range(6):
            base = FROM_N if g == 0 else FROM_S if g == 5 else OWN + 3 * (g - 1)
            three = [EB[slot, base + k] for k in range(3)]
            values = unpack_group(three, lane)
            if g in (0, 5):
                values = [jnp.where(deep, values[i], three[i % 2]) for i in range(4)]
            mask = in_lanes
            if g == 0:
                mask = mask * jnp.where(at_top, 0.0, 1.0)
            if g == 5:
                mask = mask * jnp.where(at_bottom, 0.0, 1.0)
            for i in range(4):
                e, w = 2 * g + i // 2, i % 2
                from_left, from_right, rb = halo_at(e)
                q = rb * 2 + w
                value = jnp.where(lane < LOW, roll(from_left, LOW - 8 - 8 * q, 1), values[i])
                value = jnp.where(lane >= HIGH, roll(from_right, HIGH - 8 * q, 1), value)
                NB[w, 8 * e:8 * e + 8, :] = value * mask
        for t in range(T_CHAIN):
            for w in range(2):
                store(t, w, NB[w, pl.ds(t, 8, stride=T_CHAIN), :])

    chain_rows = {15 % T_CHAIN: strip_mask(15 // T_CHAIN, at_top), 80 % T_CHAIN: strip_mask(80 // T_CHAIN, at_bottom)}
    share = pltpu.make_async_remote_copy(
        CB, CN, send_share, recv_share, (jnp.maximum(me - 1, 0), row, col), MESH)

    def natural(ref):
        for t in range(T_CHAIN):
            for w in range(2):
                NB[w, pl.ds(t, 8, stride=T_CHAIN), :] = V12[t, w]
        for w in range(2):
            ref[w] = NB[w, 16:16 + CROWS, :]

    def relaxed_base():
        await_vectors(RX, recv_relaxed)
        for rb in range(16):
            values = unpack_group([RX[k, 8 * rb:8 * rb + 8, :] for k in range(3)], lane)
            for w in range(4):
                RN[w, 8 * rb:8 * rb + 8, :] = values[w]
        for t in range(8):
            for w in range(2):
                def at(tt, ww):
                    return RN[ww, pl.ds(tt, 8, stride=16), :]
                RR[t, w] = 0.25 * ((at(2 * t, 2 * w) + at(2 * t, 2 * w + 1)) + (at(2 * t + 1, 2 * w) + at(2 * t + 1, 2 * w + 1)))
        base = move_columns(jnp.concatenate([RX[k] for k in range(3)], axis=1), GATHER[...])
        for k in range(3):
            BASE[k] = base[:, 128 * k:128 * k + 128]

    @pl.when(core == 1)
    def _():
        def put(ref):
            def store(t, w, x):
                ref[t, w] = x
            return store

        await_vectors(EB.at[7:9, FROM_N:SLOT], recv3.at[7])
        unpack(7, put(C12))
        unpack(8, put(S12))

    relaxed_base()

    @pl.when(core == 1)
    def _():
        def put(t, w, x):
            V12[t, w] = x

        def add(t, w, x):
            V12[t, w] = V12[t, w] + x

        @pl.when(is_last)
        def _():
            for v in range(12):
                EB[0, v] = SB[0, v]
            await_vectors(EB.at[0, FROM_N:SLOT], recv3.at[0])

        @pl.when(me == 1)
        def _():
            await_vectors(EB.at[0, 0:FROM_N], recv3.at[0])

        @pl.when(jnp.logical_and(me != last, me > 1))
        def _():
            await_vectors(EB.at[0, 0:SHALLOW], recv3.at[0])

        unpack(0, put, is_last)

        @pl.when(me > 1)
        def _():
            heun(V12, A12, C12, S12, T_CHAIN, 2, in_lanes, chain_rows)

            @pl.when(is_last)
            def _():
                await_vectors(EB.at[1], recv3.at[1])

            @pl.when(jnp.logical_not(is_last))
            def _():
                await_vectors(EB.at[1, 0:SHALLOW], recv3.at[1])

            unpack(1, add, is_last)

        def body(slot, carry):
            final = slot == me - 1

            @pl.when(final)
            def _():
                natural(CB)
                share.start()
                await_vectors(EB.at[slot, 0:FROM_N], recv3.at[slot])

            @pl.when(jnp.logical_not(final))
            def _():
                await_vectors(EB.at[slot, 0:SHALLOW], recv3.at[slot])

            heun(V12, A12, C12, S12, T_CHAIN, 2, in_lanes, chain_rows)
            unpack(slot, add, False)
            return carry

        lax.fori_loop(2, me, body, 0)
        natural(CN)

        @pl.when(me > 1)
        def _():
            share.wait_send()

    @pl.when(jnp.logical_and(core == 0, me > 0))
    def _():
        share.wait_recv()

    @pl.when(me == 0)
    def _():
        for t in range(8):
            for w in range(2):
                CN[w, pl.ds(t, 8, stride=8), :] = RR[t, w]

    change = jnp.concatenate(
        [jnp.concatenate([jnp.where(own_lanes, CN[w, pl.ds(t, 8, stride=8), :] - RR[t, w], 0.0) for w in range(2)], axis=1)
         for t in range(8)], axis=0)
    change = move_columns(change, PROLONG[...])
    for k in range(3):
        for t in range(8):
            for tt in (2 * t, 2 * t + 1):
                OUT[k, pl.ds(tt, 8, stride=16), :] = (
                    BASE[k, pl.ds(tt, 8, stride=16), :] + change[8 * t:8 * t + 8, 128 * k:128 * k + 128])
        out[0, :, 128 * k:128 * k + 128] = OUT[k]

    await_vectors(R1, send1)

    @pl.when(core == 1)
    def _():
        await_vectors(EB.at[7:9, FROM_N:SLOT], send_coef)

    relaxed_copy.wait_send()
    each_receiver(finish)


def local(initial, guesses, conduct, source):
    nt = lax.axis_size("tm")
    f32, bf16 = jnp.float32, jnp.bfloat16
    vmem, dma = pltpu.VMEM, pltpu.SemaphoreType.DMA
    fine, coarse, chain = (T_FINE, 4, 8, 128), (T_COARSE, 2, 8, 128), (T_CHAIN, 2, 8, 128)
    scratch = [
        vmem((3, ROWS, COLS), f32),
        vmem((3, 4, EXT, 128), f32),
        vmem((3, EXT, 128), f32),
        vmem((2, 18, 8, 128), f32),
        vmem((2, 4, 3, 8, 128), f32),
        vmem((2, 2, 8, 128), f32),
        vmem((R_ALL, 8, 128), f32),
        vmem(fine, f32),
        vmem(fine, f32),
        vmem(fine, f32),
        vmem(fine, f32),
        vmem((COLS, 512), bf16),
        vmem((COLS, COLS), bf16),
        vmem((256, COLS), bf16),
        vmem((4, EXT, 128), f32),
        vmem((3, ROWS, 128), f32),
        vmem((3, ROWS, 128), f32),
        vmem((8, 2, 8, 128), f32),
        vmem((3, ROWS, 128), f32),
        vmem(coarse, f32),
        vmem(coarse, f32),
        vmem(coarse, f32),
        vmem(coarse, f32),
        vmem((3, 2, EXT // 2, 128), f32),
        vmem((3, 18, 8, 128), f32),
        vmem((3, 4, 2, 128), f32),
        vmem((9, SLOT, 8, 128), f32),
        vmem((9, 4, 2, 128), f32),
        vmem((2, CROWS + 32, 128), f32),
        vmem(chain, f32),
        vmem(chain, f32),
        vmem(chain, f32),
        vmem(chain, f32),
        vmem((2, CROWS, 128), f32),
        vmem((2, CROWS, 128), f32),
        vmem((3, ROWS, 128), f32),
        dma, dma, dma((2,)), dma, dma, dma((nt // 2,)), dma((8,)), dma, dma, dma,
        pltpu.SemaphoreType.REGULAR,
    ]
    return pl.pallas_call(
        kernel,
        out_shape=jax.ShapeDtypeStruct(guesses.shape, f32),
        in_specs=[pl.BlockSpec(memory_space=pl.ANY)] * 4,
        out_specs=pl.BlockSpec(memory_space=pltpu.VMEM),
        scratch_shapes=scratch,
        compiler_params=pltpu.CompilerParams(collective_id=0, has_side_effects=True, vmem_limit_bytes=54976 * 1024),
    )(initial, guesses, conduct, source)


def solution(mesh):
    in_specs = (P("sx", "sy"), P("tm", "sx", "sy"), P("sx", "sy"), P("sx", "sy"))
    out_specs = P("tm", "sx", "sy")
    return jax.shard_map(local, mesh=mesh, in_specs=in_specs, out_specs=out_specs, check_vma=False)
```

```python
import jax
import jax.numpy as jnp
from jax import lax
from jax.experimental import pallas as pl
from jax.experimental.pallas import tpu as pltpu
from jax.sharding import PartitionSpec as P

MESH = pl.DeviceIdType.MESH
FINE = 4
TIME_STEP = 0.035

ROWS, COLS, HALO = 128, 384, 16
EXT = ROWS + 2 * HALO
T_FINE = EXT // 8
T_COARSE = T_FINE // 2
CROWS = ROWS // 2
T_CHAIN = (CROWS + 32) // 8
LOW, HIGH = 16, 112
OWN, FROM_N, FROM_S, FROM_L, FROM_R, SLOT, SHALLOW = 0, 12, 15, 18, 19, 21, 19
FROM_NL, FROM_NR, FROM_SL, FROM_SR = range(4)
R_N, R_S, R_L, R_R, R_NL, R_NR, R_SL, R_SR, R_ALL = 0, 18, 36, 48, 60, 61, 62, 63, 64


def roll(x, shift, axis):
    shift = shift % x.shape[axis]
    return pltpu.roll(x, shift, axis) if shift else x


def flux_pass(src, coef, drift, T, W, emit):
    def load(t):
        values = [src[t, w] for w in range(W)]
        return values, [coef[t, w] * (2.0 + jnp.tanh(values[w])) for w in range(W)]

    def flux(v, k, vn, kn):
        return (k + kn) * (vn - v)

    first, last = load(0), load(T - 1)
    final = [flux(last[0][w], last[1][w], roll(first[0][w], -1, 0), roll(first[1][w], -1, 0)) for w in range(W)]
    above = [roll(f, 1, 0) for f in final]
    here = first
    for t in range(T):
        v, k = here
        if t < T - 1:
            following = last if t + 1 == T - 1 else load(t + 1)
            below = [flux(v[w], k[w], following[0][w], following[1][w]) for w in range(W)]
        else:
            following, below = None, final
        east = [flux(v[w], k[w], v[w + 1], k[w + 1]) for w in range(W - 1)]
        east.append(flux(v[W - 1], k[W - 1], roll(v[0], -1, 1), roll(k[0], -1, 1)))
        west = [roll(east[W - 1], 1, 1)] + east[:-1]
        for w in range(W):
            emit(t, w, v[w], drift[t, w] + ((east[w] - west[w]) + (below[w] - above[w])))
        here, above = following, below


def heun(state, section, coef, drift, T, W, lanes, row_masks, emit=None):
    def keep(t, w, x):
        if w in (0, W - 1):
            x = x * lanes
        if t in row_masks:
            x = x * row_masks[t]
        return x

    def first(t, w, value, increment):
        middle = value + increment
        state[t, w] = middle
        section[t, w] = keep(t, w, middle + increment)

    def second(t, w, value, increment):
        result = keep(t, w, state[t, w] + increment)
        if emit is None:
            state[t, w] = result
        else:
            emit(t, w, result)

    flux_pass(state, coef, drift, T, W, first)
    flux_pass(section, coef, drift, T, W, second)


def pieces(x):
    top = x.astype(jnp.bfloat16)
    rest = x - top.astype(jnp.float32)
    middle = rest.astype(jnp.bfloat16)
    low = (rest - middle.astype(jnp.float32)).astype(jnp.bfloat16)
    return top, middle, low


def move_columns(x, choice):
    moved = jnp.dot(jnp.concatenate(pieces(x), axis=0), choice, preferred_element_type=jnp.float32)
    n = x.shape[0]
    return (moved[:n] + moved[n:2 * n]) + moved[2 * n:]


def skew(x, step, sublane):
    moved = [roll(x, step * k, 1) for k in range(4)]
    i = sublane & 3
    return jnp.where(i < 2, jnp.where(i == 0, moved[0], moved[1]), jnp.where(i == 2, moved[2], moved[3]))


def pack_group(x, own):
    return [jnp.where(own, x[k], roll(x[3], 96 - 32 * k, 1)) for k in range(3)]


def unpack_group(y, lane):
    parts = [roll(y[k], 32 * k - 96, 1) for k in range(3)]
    return list(y) + [jnp.where(lane < LOW + 32, parts[0], jnp.where(lane < LOW + 64, parts[1], parts[2]))]


def kernel(
    initial, guesses, conduct, source, out,
    X, Y, HX, SR, SC, SK, R1, V, A, CH, SD, SPREAD, GATHER, PROLONG, RN, RS, RX, RR, BASE, RV, CA, CC, CSD, NAT, SB, SE, EB, EE, NB,
    V12, A12, C12, S12, CN, CB, OUT,
    load_sem, store_sem, send1, recv1, send_relaxed, recv_relaxed, send3, recv3, send_coef, send_share, recv_share, ready,
):
    nt, nx, ny = lax.axis_size("tm"), lax.axis_size("sx"), lax.axis_size("sy")
    me, row, col = lax.axis_index("tm"), lax.axis_index("sx"), lax.axis_index("sy")
    chip, core = me // 2, lax.rem(me, 2)
    chips, last = nt // 2, nt - 1
    north, south = lax.rem(row + nx - 1, nx), lax.rem(row + 1, nx)
    left, right = lax.rem(col + ny - 1, ny), lax.rem(col + 1, ny)
    spatial = [(north, col), (south, col), (row, left), (row, right),
               (north, left), (north, right), (south, left), (south, right)]

    barrier = pltpu.get_barrier_semaphore()
    for r, c in spatial:
        pl.semaphore_signal(barrier, inc=1, device_id=(me, r, c), device_id_type=MESH)
    for step in range(1, nt):
        pl.semaphore_signal(barrier, inc=1, device_id=(lax.rem(me + step, nt), row, col), device_id_type=MESH)

    def await_vectors(ref, sem):
        pltpu.make_async_copy(ref, ref, sem).wait()

    @pl.when(me == last)
    def _():
        pltpu.make_async_copy(initial, X.at[0], load_sem).start()

    @pl.when(me != last)
    def _():
        pltpu.make_async_copy(guesses.at[0], X.at[0], load_sem).start()

    pltpu.make_async_copy(conduct, X.at[1], load_sem).start()
    pltpu.make_async_copy(source, X.at[2], load_sem).start()

    lane = lax.broadcasted_iota(jnp.int32, (8, 128), 1)
    sublane = lax.broadcasted_iota(jnp.int32, (8, 128), 0)
    one, zero = jnp.ones((8, 128), jnp.float32), jnp.zeros((8, 128), jnp.float32)
    own_lanes = jnp.logical_and(lane >= LOW, lane < HIGH)
    at_top, at_bottom, at_left, at_right = row == 0, row == nx - 1, col == 0, col == ny - 1
    in_lanes = jnp.where(jnp.logical_or(jnp.logical_and(lane < LOW, at_left), jnp.logical_and(lane >= HIGH, at_right)), zero, one)

    def strip_mask(which, edge):
        return jnp.where(jnp.logical_and(sublane == which, edge), zero, one)

    def fill(ref, rows, columns):
        ref[...] = jnp.where(rows == columns, 1.0, 0.0).astype(jnp.bfloat16)

    o = lax.broadcasted_iota(jnp.int32, (1, 512), 1)
    fill(SPREAD, lax.broadcasted_iota(jnp.int32, (COLS, 1), 0) + 64, (o & 127) * 4 + (o >> 7))
    o = lax.broadcasted_iota(jnp.int32, (COLS, 1), 0)
    k, l = o >> 7, o & 127
    inside = jnp.logical_and(l >= LOW, l < HIGH)
    packed_from = jnp.where(inside, 4 * l + k, 4 * (((l + 16) & 127) + LOW + 32 * k) + 3)
    fill(GATHER, packed_from, lax.broadcasted_iota(jnp.int32, (1, COLS), 1) + 64)
    o = lax.broadcasted_iota(jnp.int32, (256, 1), 0)
    fill(PROLONG, (o & 127) * 2 + (o >> 7), (lax.broadcasted_iota(jnp.int32, (1, COLS), 1) + 64) >> 1)

    pltpu.make_async_copy(X, X, load_sem).wait()

    for field, factor in ((0, None), (1, 0.125 * TIME_STEP), (2, 0.5 * TIME_STEP)):
        spread = move_columns(X[field], SPREAD[...])
        for w in range(4):
            part = spread[:, 128 * w:128 * w + 128]
            Y[field, w, HALO:HALO + ROWS, :] = part if factor is None else part * factor

    def own_block(field, w, rb):
        return Y[field, w, HALO + 8 * rb:HALO + 8 * rb + 8, :]

    for field in range(3):
        for side in range(2):
            for b in range(2):
                packed = pack_group([own_block(field, w, b if side == 0 else 14 + b) for w in range(4)], own_lanes)
                for k in range(3):
                    SR[side, field * 6 + b * 3 + k] = packed[k]
    eighth = lane // 8
    for field in range(3):
        for side in range(2):
            for quarter in range(4):
                packed = None
                for q in range(16):
                    block = own_block(field, q % 4, 4 * quarter + q // 4)
                    block = roll(block, 8 * q + 100 - LOW if side == 0 else 8 * q - (HIGH - 4), 1)
                    slot_of = (q + 12) % 16 if side == 0 else q
                    packed = block if packed is None else jnp.where(eighth == slot_of, block, packed)
                SC[side, quarter, field] = packed
    odd_slot = (lane & 4) != 0
    for side in range(2):
        for end, quarter in ((0, 0), (1, 3)):
            fields = [SC[side, quarter, field] for field in range(3)]
            if side == 1:
                half = (lane < 64) if end == 0 else (lane >= 64)
                pair = jnp.where(odd_slot, roll(fields[1], 4, 1), fields[0])
            else:
                half = ((lane + 32) & 127) < 64 if end == 0 else ((lane + 32) & 127) >= 64
                pair = jnp.where(odd_slot, fields[0], roll(fields[1], -4, 1))
            SK[side, end] = jnp.where(half, pair, roll(fields[2], 64, 1))

    def pack_coarse(which):
        def block(rb, w):
            return NAT[which, w, 8 + 8 * rb:16 + 8 * rb, :]

        for g in range(4):
            packed = pack_group([block(2 * g + i // 2, i % 2) for i in range(4)], own_lanes)
            for k in range(3):
                SB[which, 3 * g + k] = packed[k]
        for w in range(2):
            SB[which, 14 + w] = block(0, w)
            SB[which, 16 + w] = block(7, w)
        for side in range(2):
            packed = None
            for q in range(16):
                moved = roll(block(q // 2, q % 2), 8 * q - LOW if side == 0 else 8 * q - (HIGH - 8), 1)
                packed = moved if packed is None else jnp.where(eighth == q, moved, packed)
            SB[which, 12 + side] = packed
            for end in range(2):
                moved = skew(roll(packed, 32 if end else 0, 1), 32, sublane)
                moved = jnp.where((lane // 32) == (sublane & 3), moved, 0.0)
                moved = moved + roll(moved, 1, 0)
                moved = moved + roll(moved, 2, 0)
                SE[which, 2 * side + end, 0:1, :] = moved[3:4, :]
                SE[which, 2 * side + end, 1:2, :] = moved[7:8, :]

    def coarse_copies(which, slot, tm, send, recv, deep=True):
        def copy(src, dst, where):
            return pltpu.make_async_remote_copy(src, dst, send, recv, (tm,) + where, MESH)

        def vectors(a, size, k, where):
            return copy(SB.at[which, a:a + size], EB.at[slot, k:k + size], where)

        return [
            copy(SE.at[which, 0], EE.at[slot, FROM_SR], (north, left)),
            copy(SE.at[which, 2], EE.at[slot, FROM_SL], (north, right)),
            copy(SE.at[which, 1], EE.at[slot, FROM_NR], (south, left)),
            copy(SE.at[which, 3], EE.at[slot, FROM_NL], (south, right)),
            vectors(0, 3, FROM_S, (north, col)) if deep else vectors(14, 2, FROM_S, (north, col)),
            vectors(9, 3, FROM_N, (south, col)) if deep else vectors(16, 2, FROM_N, (south, col)),
            vectors(12, 1, FROM_R, (row, left)),
            vectors(13, 1, FROM_L, (row, right)),
            vectors(0, 12, OWN, (row, col)),
        ]

    coef_copies = [copy for k in (1, 2) for copy in coarse_copies(k, 6 + k, me, send_coef, recv3.at[7])[:8]]

    @pl.when(core == 1)
    def _():
        for k in (1, 2):
            for rb in range(8):
                for w in range(2):
                    def at(ww, r):
                        return Y[k, ww, pl.ds(HALO + 16 * rb + r, 8, stride=2), :]
                    total = (at(2 * w, 0) + at(2 * w + 1, 0)) + (at(2 * w, 1) + at(2 * w + 1, 1))
                    NAT[k, w, 8 + 8 * rb:16 + 8 * rb, :] = 0.25 * total if k == 1 else total
            pack_coarse(k)
            for v in range(12):
                EB[6 + k, v] = SB[k, v]

    pl.semaphore_wait(barrier, 8 + nt - 1)

    first_exchange = [
        pltpu.make_async_remote_copy(s, R1.at[k:k + size], send1, recv1, (me,) + w, MESH)
        for s, k, size, w in [
            (SK.at[1, 1:2], R_NL, 1, (south, right)),
            (SK.at[0, 1:2], R_NR, 1, (south, left)),
            (SK.at[1, 0:1], R_SL, 1, (north, right)),
            (SK.at[0, 0:1], R_SR, 1, (north, left)),
            (SR.at[0], R_S, 18, (north, col)),
            (SR.at[1], R_N, 18, (south, col)),
        ]
    ]
    for side, k, w in ((1, R_L, (row, right)), (0, R_R, (row, left))):
        for quarter in range(4):
            first_exchange.append(pltpu.make_async_remote_copy(
                SC.at[side, quarter], R1.at[k + 3 * quarter:k + 3 * quarter + 3], send1, recv1, (me,) + w, MESH))
    for copy in first_exchange:
        copy.start()

    @pl.when(core == 1)
    def _():
        for copy in coef_copies:
            copy.start()

    pltpu.make_async_copy(R1, R1, recv1).wait()

    for step in range(1, nt):
        pl.semaphore_signal(ready, inc=1, device_id=(lax.rem(me + step, nt), row, col), device_id_type=MESH)

    top16, bottom16 = strip_mask(0, at_top), strip_mask(7, at_bottom)
    masks = [in_lanes * (top16 if t < HALO else 1.0) * (bottom16 if t >= T_FINE - HALO else 1.0) for t in range(T_FINE)]
    for field, dest in ((1, CH), (0, V), (2, SD)):
        halo = {}
        for e in range(EXT // 8):
            if e < 2:
                l, r, rb = R_NL, R_NR, 14 + e
            elif e >= 18:
                l, r, rb = R_SL, R_SR, e - 18
            else:
                rb = e - 2
                l, r = R_L + 3 * (rb // 4), R_R + 3 * (rb // 4)
            if (l, r) not in halo:
                if e < 2 or e >= 18:
                    shift = (0, 4, 64)[field]
                    halo[l, r] = jnp.where(odd_slot, roll(R1[r], shift, 1), roll(R1[l], -shift, 1))
                else:
                    halo[l, r] = jnp.where(odd_slot, R1[r + field], R1[l + field])
            if e < 2 or e >= 18:
                start = (R_N + e * 3 if e < 2 else R_S + (e - 18) * 3) + field * 6
                values = unpack_group([R1[start + k] for k in range(3)], lane)
                for w in range(4):
                    Y[field, w, 8 * e:8 * e + 8, :] = values[w]
            HX[field, 8 * e:8 * e + 8, :] = roll(halo[l, r], -32 * (rb % 4), 1)
        for t in range(T_FINE):
            around = HX[field, pl.ds(t, 8, stride=T_FINE), :]
            for w in range(4):
                value = Y[field, w, pl.ds(t, 8, stride=T_FINE), :]
                dest[t, w] = jnp.where(own_lanes, value, roll(around, LOW - 4 - 8 * w, 1)) * masks[t]

    def four(ref, t, w):
        return (ref[2 * t, 2 * w] + ref[2 * t, 2 * w + 1]) + (ref[2 * t + 1, 2 * w] + ref[2 * t + 1, 2 * w + 1])

    for t in range(T_COARSE):
        for w in range(2):
            CC[t, w] = 0.25 * four(CH, t, w)
            CSD[t, w] = four(SD, t, w)

    fine_rows = {HALO - 1: top16, T_FINE - HALO: bottom16}

    def fine_run():
        def body(i, carry):
            heun(V, A, CH, SD, T_FINE, 4, in_lanes, fine_rows)
            return carry

        lax.fori_loop(0, FINE, body, 0)

    fine_run()

    for t in range(T_FINE):
        for w in range(4):
            RN[w, pl.ds(t, 8, stride=T_FINE), :] = V[t, w]
    for rb in range(16):
        packed = pack_group([RN[w, HALO + 8 * rb:HALO + 8 * rb + 8, :] for w in range(4)], own_lanes)
        for k in range(3):
            RS[k, 8 * rb:8 * rb + 8, :] = packed[k]
    relaxed_copy = pltpu.make_async_remote_copy(
        RS, RX, send_relaxed, recv_relaxed, (lax.rem(me + 1, nt), row, col), MESH)
    relaxed_copy.start()
    for t in range(T_COARSE):
        for w in range(2):
            RV[t, w] = 0.25 * four(V, t, w)

    fine_run()

    share_of_psi = jnp.where(me == last, 0.0, 1.0)

    def target(t, w, result):
        NAT[0, w, pl.ds(t, 8, stride=T_COARSE), :] = 0.25 * four(V, t, w) - share_of_psi * result

    coarse_rows = {HALO // 2 - 1: top16, T_COARSE - HALO // 2: bottom16}
    heun(RV, CA, CC, CSD, T_COARSE, 2, in_lanes, coarse_rows, target)
    pack_coarse(0)
    pl.semaphore_wait(ready, nt - 1)

    slot_out = jnp.where(me == last, 0, me + 1)
    is_last = me == last

    def each_receiver(action):
        for k in (0, 3, 2, 1):
            shallow, deep = [
                coarse_copies(0, slot_out, 2 * lax.rem(chip + k, chips) + 1, send3.at[k], recv3.at[slot_out], deep)
                for deep in (False, True)]
            if k == 0:
                @pl.when(is_last)
                def _():
                    action(k, deep[:8], SLOT - FROM_N)
                continue
            reached = jnp.logical_or(is_last, jnp.logical_and(chip + k < chips, me < last - 1))
            special = me == 0 if k == 3 else core == 1 if k == 1 else None

            @pl.when(reached if special is None else jnp.logical_and(reached, jnp.logical_not(special)))
            def _():
                action(k, shallow, SHALLOW)

            if special is not None:
                @pl.when(jnp.logical_and(reached, special))
                def _():
                    if k == 3:
                        action(k, deep, SLOT)
                    else:
                        action(k, shallow[8:], FROM_N)

    def start(k, copies, vectors):
        for copy in copies:
            copy.start()

    def finish(k, copies, vectors):
        await_vectors(EB.at[0, 0:vectors], send3.at[k])

    each_receiver(start)

    def unpack(slot, store, deep=True):
        def halo_at(e):
            if e < 2:
                return corners[FROM_NL], corners[FROM_NR], e
            if e >= 10:
                return corners[FROM_SL], corners[FROM_SR], e - 10
            return EB[slot, FROM_L], EB[slot, FROM_R], e - 2

        corners = []
        for k in range(4):
            two = jnp.where(sublane < 4, EE[slot, k, 0:1, :], EE[slot, k, 1:2, :])
            corners.append(skew(two, -32, sublane))

        for g in range(6):
            base = FROM_N if g == 0 else FROM_S if g == 5 else OWN + 3 * (g - 1)
            three = [EB[slot, base + k] for k in range(3)]
            values = unpack_group(three, lane)
            if g in (0, 5):
                values = [jnp.where(deep, values[i], three[i % 2]) for i in range(4)]
            mask = in_lanes
            if g == 0:
                mask = mask * jnp.where(at_top, 0.0, 1.0)
            if g == 5:
                mask = mask * jnp.where(at_bottom, 0.0, 1.0)
            for i in range(4):
                e, w = 2 * g + i // 2, i % 2
                from_left, from_right, rb = halo_at(e)
                q = rb * 2 + w
                value = jnp.where(lane < LOW, roll(from_left, LOW - 8 - 8 * q, 1), values[i])
                value = jnp.where(lane >= HIGH, roll(from_right, HIGH - 8 * q, 1), value)
                NB[w, 8 * e:8 * e + 8, :] = value * mask
        for t in range(T_CHAIN):
            for w in range(2):
                store(t, w, NB[w, pl.ds(t, 8, stride=T_CHAIN), :])

    chain_rows = {15 % T_CHAIN: strip_mask(15 // T_CHAIN, at_top), 80 % T_CHAIN: strip_mask(80 // T_CHAIN, at_bottom)}
    share = pltpu.make_async_remote_copy(
        CB, CN, send_share, recv_share, (jnp.maximum(me - 1, 0), row, col), MESH)

    def natural(ref):
        for t in range(T_CHAIN):
            for w in range(2):
                NB[w, pl.ds(t, 8, stride=T_CHAIN), :] = V12[t, w]
        for w in range(2):
            ref[w] = NB[w, 16:16 + CROWS, :]

    def relaxed_base():
        await_vectors(RX, recv_relaxed)
        for rb in range(16):
            values = unpack_group([RX[k, 8 * rb:8 * rb + 8, :] for k in range(3)], lane)
            for w in range(4):
                RN[w, 8 * rb:8 * rb + 8, :] = values[w]
        for t in range(8):
            for w in range(2):
                def at(tt, ww):
                    return RN[ww, pl.ds(tt, 8, stride=16), :]
                RR[t, w] = 0.25 * ((at(2 * t, 2 * w) + at(2 * t, 2 * w + 1)) + (at(2 * t + 1, 2 * w) + at(2 * t + 1, 2 * w + 1)))
        base = move_columns(jnp.concatenate([RX[k] for k in range(3)], axis=1), GATHER[...])
        for k in range(3):
            BASE[k] = base[:, 128 * k:128 * k + 128]

    @pl.when(core == 1)
    def _():
        def put(ref):
            def store(t, w, x):
                ref[t, w] = x
            return store

        await_vectors(EB.at[7:9, FROM_N:SLOT], recv3.at[7])
        unpack(7, put(C12))
        unpack(8, put(S12))

    relaxed_base()

    @pl.when(core == 1)
    def _():
        def put(t, w, x):
            V12[t, w] = x

        def add(t, w, x):
            V12[t, w] = V12[t, w] + x

        @pl.when(is_last)
        def _():
            for v in range(12):
                EB[0, v] = SB[0, v]
            await_vectors(EB.at[0, FROM_N:SLOT], recv3.at[0])

        @pl.when(me == 1)
        def _():
            await_vectors(EB.at[0, 0:FROM_N], recv3.at[0])

        @pl.when(jnp.logical_and(me != last, me > 1))
        def _():
            await_vectors(EB.at[0, 0:SHALLOW], recv3.at[0])

        unpack(0, put, is_last)

        @pl.when(me > 1)
        def _():
            heun(V12, A12, C12, S12, T_CHAIN, 2, in_lanes, chain_rows)

            @pl.when(is_last)
            def _():
                await_vectors(EB.at[1], recv3.at[1])

            @pl.when(jnp.logical_not(is_last))
            def _():
                await_vectors(EB.at[1, 0:SHALLOW], recv3.at[1])

            unpack(1, add, is_last)

        def body(slot, carry):
            final = slot == me - 1

            @pl.when(final)
            def _():
                natural(CB)
                share.start()
                await_vectors(EB.at[slot, 0:FROM_N], recv3.at[slot])

            @pl.when(jnp.logical_not(final))
            def _():
                await_vectors(EB.at[slot, 0:SHALLOW], recv3.at[slot])

            heun(V12, A12, C12, S12, T_CHAIN, 2, in_lanes, chain_rows)
            unpack(slot, add, False)
            return carry

        lax.fori_loop(2, me, body, 0)
        natural(CN)

        @pl.when(me > 1)
        def _():
            share.wait_send()

    @pl.when(jnp.logical_and(core == 0, me > 0))
    def _():
        share.wait_recv()

    @pl.when(me == 0)
    def _():
        for t in range(8):
            for w in range(2):
                CN[w, pl.ds(t, 8, stride=8), :] = RR[t, w]

    change = jnp.concatenate(
        [jnp.concatenate([jnp.where(own_lanes, CN[w, pl.ds(t, 8, stride=8), :] - RR[t, w], 0.0) for w in range(2)], axis=1)
         for t in range(8)], axis=0)
    change = move_columns(change, PROLONG[...])
    for k in range(3):
        for t in range(8):
            for tt in (2 * t, 2 * t + 1):
                OUT[k, pl.ds(tt, 8, stride=16), :] = (
                    BASE[k, pl.ds(tt, 8, stride=16), :] + change[8 * t:8 * t + 8, 128 * k:128 * k + 128])
        pltpu.make_async_copy(OUT.at[k], out.at[0, :, 128 * k:128 * k + 128], store_sem).start()

    await_vectors(R1, send1)

    @pl.when(core == 1)
    def _():
        await_vectors(EB.at[7:9, FROM_N:SLOT], send_coef)

    relaxed_copy.wait_send()
    each_receiver(finish)
    await_vectors(OUT, store_sem)


def local(initial, guesses, conduct, source):
    nt = lax.axis_size("tm")
    f32, bf16 = jnp.float32, jnp.bfloat16
    vmem, dma = pltpu.VMEM, pltpu.SemaphoreType.DMA
    fine, coarse, chain = (T_FINE, 4, 8, 128), (T_COARSE, 2, 8, 128), (T_CHAIN, 2, 8, 128)
    scratch = [
        vmem((3, ROWS, COLS), f32),
        vmem((3, 4, EXT, 128), f32),
        vmem((3, EXT, 128), f32),
        vmem((2, 18, 8, 128), f32),
        vmem((2, 4, 3, 8, 128), f32),
        vmem((2, 2, 8, 128), f32),
        vmem((R_ALL, 8, 128), f32),
        vmem(fine, f32),
        vmem(fine, f32),
        vmem(fine, f32),
        vmem(fine, f32),
        vmem((COLS, 512), bf16),
        vmem((COLS, COLS), bf16),
        vmem((256, COLS), bf16),
        vmem((4, EXT, 128), f32),
        vmem((3, ROWS, 128), f32),
        vmem((3, ROWS, 128), f32),
        vmem((8, 2, 8, 128), f32),
        vmem((3, ROWS, 128), f32),
        vmem(coarse, f32),
        vmem(coarse, f32),
        vmem(coarse, f32),
        vmem(coarse, f32),
        vmem((3, 2, EXT // 2, 128), f32),
        vmem((3, 18, 8, 128), f32),
        vmem((3, 4, 2, 128), f32),
        vmem((9, SLOT, 8, 128), f32),
        vmem((9, 4, 2, 128), f32),
        vmem((2, CROWS + 32, 128), f32),
        vmem(chain, f32),
        vmem(chain, f32),
        vmem(chain, f32),
        vmem(chain, f32),
        vmem((2, CROWS, 128), f32),
        vmem((2, CROWS, 128), f32),
        vmem((3, ROWS, 128), f32),
        dma, dma, dma, dma, dma, dma, dma((nt // 2,)), dma((8,)), dma, dma, dma,
        pltpu.SemaphoreType.REGULAR,
    ]
    return pl.pallas_call(
        kernel,
        out_shape=jax.ShapeDtypeStruct(guesses.shape, f32),
        in_specs=[pl.BlockSpec(memory_space=pl.ANY)] * 4,
        out_specs=pl.BlockSpec(memory_space=pl.ANY),
        scratch_shapes=scratch,
        compiler_params=pltpu.CompilerParams(collective_id=0, has_side_effects=True, vmem_limit_bytes=54976 * 1024),
    )(initial, guesses, conduct, source)


def solution(mesh):
    in_specs = (P("sx", "sy"), P("tm", "sx", "sy"), P("sx", "sy"), P("sx", "sy"))
    out_specs = P("tm", "sx", "sy")
    return jax.shard_map(local, mesh=mesh, in_specs=in_specs, out_specs=out_specs, check_vma=False)
```
